32 devices in a mesh: bx: 4 (over y, x), by: 8 (over z, core).
Axes of the slice: x: 2, y: 2, z: 4, core: 2. Of those that a mesh axis runs over, the one named last changes fastest.
Arguments:
- views: float32 [3, 2, 64, 256, 128], P(None, None, 'bx', 'by'), may hold values from 0.2 to 3
- estimate: float32 [2, 64, 256, 128], P(None, 'bx', 'by'), may hold values from 0.5 to 2
- profiles: float32 [4, 8, 3, 256, 128], P('bx', 'by'), may hold values from 0.3 to 1
- kernels: float32 [3, 3, 31], replicated, may hold values from 0.004 to 0.06
- owners: int32 [3, 4], replicated, may hold values from 0 to 7
Outputs:
- deconvolved: float32 [2, 64, 256, 128], P(None, 'bx', 'by')
The draws below stay inside these ranges and needn't reach their ends.
Inputs may be any that keep to these rules, and one draw needn't show every extreme that they name: `owners`: an index along the brick columns.
All inputs are finite; a program needn't handle non-finite values.
Results may differ from the reference program's by a relative error of at most 0.0001.
Values sent between devices are 32-bit elements; how exact they have to be, the bound alone decides.
No kernel may reach another device: no remote copies, remote signals or barrier semaphores. Data moves between devices by JAX's collectives and lax.ppermute only.
A program may use at most 128 MiB of HBM per device.

```python
import math
import jax
import jax.numpy as jnp
from jax import lax

CH = 2
VIEWS = 3
TAPS = 31
ITERS = 1
SX = 16
Z = 128
NX = 64
NY = 256
N_BX = 4
N_BY = 8


def set_ends(array, own_key, least, top_value):
    shape = array.shape
    place = [jax.random.randint(jax.random.fold_in(own_key, axis), (), 0, shape[axis]) for axis in range(len(shape))]
    array = array.at[tuple(place)].set(least)
    longest = shape.index(max(shape))
    place[longest] = (place[longest] + 1) % shape[longest]
    return array.at[tuple(place)].set(top_value)


def levels(key, extent, shards, low, top_value):
    level = 1.0
    for position, shards_of in shards:
        draws = jax.random.uniform(jax.random.fold_in(jax.random.fold_in(key, 6), position), (shards_of,), jnp.float32, low / len(shards), top_value / len(shards))
        level = level * jnp.repeat(jnp.exp(draws), extent[position] // shards_of).reshape((-1,) + (1,) * (len(extent) - 1 - position))
    return level


def setup_inputs(seed: int = 0) -> dict:
    streams_of = jax.random.split(jax.random.key(seed), 6)
    views = jnp.clip(jnp.exp(math.log(3.0) - 2.7080502 * jax.random.uniform(streams_of[0], (VIEWS, CH, NX, NY, Z), jnp.float32) ** levels(streams_of[0], (VIEWS, CH, NX, NY, Z), ((2, 4), (3, 8)), -0.2, 0.2)), 0.2, 3.0)
    estimate = jnp.clip(jnp.exp(math.log(2.0) - 1.3862944 * jax.random.uniform(streams_of[1], (CH, NX, NY, Z), jnp.float32) ** levels(streams_of[1], (CH, NX, NY, Z), ((1, 4), (2, 8)), -0.2, 0.2)), 0.5, 2.0)
    profiles = jnp.clip(jnp.exp(math.log(1.0) - 1.2039728 * jax.random.uniform(streams_of[2], (N_BX, N_BY, VIEWS, NY, Z), jnp.float32) ** levels(streams_of[2], (N_BX, N_BY, VIEWS, NY, Z), ((0, 4), (1, 8)), -0.2, 0.2)), 0.3, 1.0)
    kernels = jnp.clip(jnp.exp(jax.random.uniform(streams_of[3], (VIEWS, 3, TAPS), jnp.float32, math.log(0.004), math.log(0.06))), 0.004, 0.06)
    owners = set_ends(jax.random.randint(streams_of[4], (VIEWS, N_BX), 0, N_BY), jax.random.fold_in(streams_of[4], 1), 0, N_BY - 1).astype(jnp.int32)
    return {"views": views, "estimate": estimate, "profiles": profiles, "kernels": kernels, "owners": owners}


def conv_axis(volume, taps, axis):
    half = TAPS // 2
    length = volume.shape[axis]
    widths = [(0, 0)] * volume.ndim
    widths[axis] = (half, half)
    padded = jnp.pad(volume, widths)
    total = jnp.zeros_like(volume)
    for step in range(TAPS):
        total = total + taps[step] * lax.slice_in_dim(padded, step, step + length, axis=axis)
    return total


def band_matrix(taps, length):
    half = TAPS // 2
    places = jnp.arange(length, dtype=jnp.int32)
    offset = places[None, :] - places[:, None]
    picked = taps[jnp.clip(offset + half, 0, TAPS - 1)]
    return jnp.where(jnp.abs(offset) <= half, picked, jnp.float32(0.0))


def blur(volume, kern):
    volume = conv_axis(volume, kern[0], 1)
    volume = conv_axis(volume, kern[1], 2)
    band = band_matrix(kern[2], volume.shape[3])
    return jnp.dot(volume, band.T, precision=lax.Precision.HIGHEST)


def reference(views, estimate, profiles, kernels, owners):
    rows = jnp.arange(N_BX, dtype=jnp.int32)
    lights = []
    for view in range(VIEWS):
        row_profile = profiles[rows, owners[view], view]
        lights.append(jnp.repeat(row_profile, SX, axis=0)[None])
    field = estimate
    for step in range(ITERS):
        summed = jnp.zeros_like(field)
        for view in range(VIEWS):
            kern = kernels[view]
            blurred = lights[view] * blur(field, kern) + 0.05
            ratio = lights[view] * views[view] / blurred
            summed = summed + blur(ratio, kern[:, ::-1])
        field = field * summed / VIEWS
    return field
```

```python
import functools

import jax
import jax.numpy as jnp
from jax import lax
from jax.experimental import pallas as pl
from jax.experimental.pallas import tpu as pltpu
from jax.sharding import PartitionSpec as P

F32 = jnp.float32
BF16 = jnp.bfloat16
PAD = 16


def shift(value, axis, step):
    count = lax.axis_size(axis)
    pairs = [(i, i + step) for i in range(count) if 0 <= i + step < count]
    return lax.ppermute(value, axis, pairs)


def halves(value):
    high = value.astype(BF16)
    return high, (value - high.astype(F32)).astype(BF16)


def matrices(taps, y_blur, y_back, z_blur, z_back):
    views, _, count = taps.shape
    half = count // 2
    width = y_blur.shape[0] // views
    slab = y_blur.shape[1] // 3
    depth = z_blur.shape[1] // 2

    def pick(view, axis, offset):
        total = jnp.zeros(offset.shape, F32)
        for step in range(count):
            total = jnp.where(offset == step, taps[view, axis, step], total)
        return halves(total)

    def position(shape, dim):
        place = lax.broadcasted_iota(jnp.int32, shape, dim)
        low = jnp.where(place < width + PAD, place - width - PAD, place - PAD)
        return jnp.where(place < width, place, low)

    def index(shape, dim):
        return lax.broadcasted_iota(jnp.int32, shape, dim)

    highs, lows = [], []
    for view in range(views):
        shape = (width, slab)
        high, low = pick(view, 1, position(shape, 1) - index(shape, 0) + half)
        y_blur[view * width : (view + 1) * width] = jnp.concatenate([high, high, low], axis=1)
        shape = (slab, width)
        high, low = pick(view, 1, position(shape, 0) - index(shape, 1) + half)
        highs.append(high)
        lows.append(low)
        shape = (depth, depth)
        offset = index(shape, 0) - index(shape, 1) + half
        for ref, at in ((z_blur, offset), (z_back, 2 * half - offset)):
            high, low = pick(view, 2, at)
            ref[view, :depth] = jnp.concatenate([high, low], axis=1)
            ref[view, depth:] = jnp.concatenate([high, jnp.zeros_like(low)], axis=1)
    y_back[...] = jnp.concatenate(highs + highs + lows, axis=1)


def bands(kernels, width, depth):
    views = kernels.shape[0]
    slab = width + 2 * PAD
    shapes = [
        (views * width, 3 * slab),
        (slab, 3 * views * width),
        (views, 2 * depth, 2 * depth),
        (views, 2 * depth, 2 * depth),
    ]
    return pl.pallas_call(
        matrices,
        out_shape=[jax.ShapeDtypeStruct(s, BF16) for s in shapes],
        in_specs=[pl.BlockSpec(memory_space=pltpu.SMEM)],
    )(kernels)


def dot(left, right):
    return jnp.dot(left, right, preferred_element_type=F32)


def fused(
    taps, own, xlo, xhi, ylo, yhi, views, lights, y_blur, y_back, z_blur, z_back,
    s_own, s_xlo, s_xhi, s_ylo, s_yhi, wide, mid,
):
    count = views.shape[0]
    planes, width, depth = own.shape[1:]
    reach = xlo.shape[1]
    total = planes + 2 * reach
    tiles = width // 8

    def place(index):
        if index < reach:
            return xlo, s_xlo, index
        if index < reach + planes:
            return own, s_own, index - reach
        return xhi, s_xhi, index - reach - planes

    def slab(index):
        ref, _, at = place(index)
        value = jnp.concatenate([ref[0, at], ylo[0, index], yhi[0, index]], axis=0)
        high, low = halves(value)
        return jnp.concatenate([high, low, high], axis=0)

    for index in range(0, total, 2):
        pair = jnp.concatenate([slab(index), slab(index + 1)], axis=1)
        out = dot(y_blur[...], pair)
        for view in range(count):
            rows = slice(view * width, (view + 1) * width)
            wide[view, index] = out[rows, :depth]
            wide[view, index + 1] = out[rows, depth:]

    def across(step, carry):
        view, rows = step // tiles, pl.ds(pl.multiple_of(step % tiles * 8, 8), 8)
        coef = [taps[view, 0, a] for a in range(2 * reach + 1)]
        sums = [None] * planes
        for index in range(total):
            value = wide[view, index, rows, :]
            for i in range(max(0, index - 2 * reach), min(planes - 1, index) + 1):
                term = coef[index - i] * value
                sums[i] = term if sums[i] is None else sums[i] + term
        for i in range(planes):
            mid[view, i, rows, :] = sums[i]
        return carry

    lax.fori_loop(0, count * tiles, across, 0)

    group = 4
    parts = planes // group

    def through(value, matrix):
        high, low = halves(value)
        out = dot(jnp.concatenate([high, low], axis=1), matrix)
        return out[:, :depth] + out[:, depth:]

    def deep(step, carry):
        view, at = step // parts, pl.ds(step % parts * group, group)
        field = through(mid[view, at].reshape(group * width, depth), z_blur[view])
        field = field.reshape(group, width, depth)
        light = lights[view][None]
        ratio = light * views[view, 0, at] / (light * field + 0.05)
        out = through(ratio.reshape(group * width, depth), z_back[view])
        mid[view, at] = out.reshape(group, width, depth)
        return carry

    lax.fori_loop(0, count * parts, deep, 0)

    def scatter(step, carry):
        view, rows = step // tiles, pl.ds(pl.multiple_of(step % tiles * 8, 8), 8)
        coef = [taps[view, 0, a] for a in range(2 * reach + 1)]
        values = [mid[view, i, rows, :] for i in range(planes)]
        for index in range(total):
            sums = None
            for i in range(max(0, index - 2 * reach), min(planes - 1, index) + 1):
                term = coef[index - i] * values[i]
                sums = term if sums is None else sums + term
            wide[view, index, rows, :] = sums
        return carry

    lax.fori_loop(0, count * tiles, scatter, 0)

    def stack(index):
        value = jnp.concatenate([wide[view, index] for view in range(count)], axis=0)
        high, low = halves(value)
        return jnp.concatenate([high, low, high], axis=0)

    for index in range(0, total, 2):
        pair = jnp.concatenate([stack(index), stack(index + 1)], axis=1)
        out = dot(y_back[...], pair)
        for side in range(2):
            _, ref, at = place(index + side)
            cols = slice(side * depth, (side + 1) * depth)
            ref[0, at] = out[:width, cols]
            s_ylo[0, index + side] = out[width : width + PAD, cols]
            s_yhi[0, index + side] = out[width + PAD :, cols]


def brick(channel, kernels, estimate, xlo, xhi, ylo, yhi, views, lights, mats):
    count = views.shape[0]
    planes, width, depth = estimate.shape[1:]
    reach = xlo.shape[1]
    total = planes + 2 * reach

    def whole(array):
        return pl.BlockSpec(array.shape, lambda i: (0,) * array.ndim)

    shapes = [(1, planes, width, depth)] + [(1, reach, width, depth)] * 2 + [(1, total, PAD, depth)] * 2
    return pl.pallas_call(
        fused,
        grid=(1,),
        out_shape=[jax.ShapeDtypeStruct(s, F32) for s in shapes],
        in_specs=[
            pl.BlockSpec(memory_space=pltpu.SMEM),
            pl.BlockSpec((1, planes, width, depth), lambda i: (channel, 0, 0, 0)),
            whole(xlo), whole(xhi), whole(ylo), whole(yhi),
            pl.BlockSpec((count, 1, planes, width, depth), lambda i: (0, channel, 0, 0, 0)),
            whole(lights),
        ] + [whole(m) for m in mats],
        out_specs=[pl.BlockSpec(s, lambda i: (0,) * 4) for s in shapes],
        scratch_shapes=[
            pltpu.VMEM((count, total, width, depth), F32),
            pltpu.VMEM((count, planes, width, depth), F32),
        ],
        compiler_params=pltpu.CompilerParams(vmem_limit_bytes=40 * 1024 * 1024),
    )(kernels, estimate, xlo, xhi, ylo, yhi, views, lights, *mats)


def illumination(profiles, owners, width):
    row, col = lax.axis_index("bx"), lax.axis_index("by")
    cols = lax.axis_size("by")
    source = lax.dynamic_index_in_dim(owners, row, axis=1, keepdims=False)
    count, _, depth = profiles.shape
    held = jnp.where((source == col)[:, None, None], profiles, F32(0.0))
    held = held.reshape(count, cols, width, depth)
    step = 1
    while step < cols:
        held = held.reshape(count, held.shape[1] // 2, 2, width, depth)
        odd = (col // step) % 2 == 1
        kept = jnp.where(odd, held[:, :, 1], held[:, :, 0])
        sent = jnp.where(odd, held[:, :, 0], held[:, :, 1])
        held = kept + lax.ppermute(sent, "by", [(i, i ^ step) for i in range(cols)])
        step *= 2
    return held.reshape(count, width, depth)


def shards(views, estimate, profiles, kernels, owners):
    channels, planes, width, depth = estimate.shape
    reach = kernels.shape[2] // 2
    mats = bands(kernels, width, depth)
    lights = illumination(profiles[0, 0], owners, width)
    results = []
    for c in range(channels):
        mine = estimate[c : c + 1]
        xlo = shift(mine[:, planes - reach :], "bx", 1)
        xhi = shift(mine[:, :reach], "bx", -1)
        ext = jnp.concatenate([xlo, mine, xhi], axis=1)
        ylo = shift(ext[:, :, width - PAD :], "by", 1)
        yhi = shift(ext[:, :, :PAD], "by", -1)
        s_own, s_xlo, s_xhi, s_ylo, s_yhi = brick(
            c, kernels, estimate, xlo, xhi, ylo, yhi, views, lights, mats
        )
        from_above = shift(s_ylo, "by", -1)
        from_below = shift(s_yhi, "by", 1)
        rim = jnp.concatenate([from_below, from_above], axis=2)
        low = s_xlo + rim[:, :reach]
        high = s_xhi + rim[:, reach + planes :]
        from_next = shift(low, "bx", -1)
        from_last = shift(high, "bx", 1)
        summed = s_own + rim[:, reach : reach + planes]
        nothing = jnp.zeros((1, planes - reach, width, depth), F32)
        summed = summed + jnp.concatenate([from_last, nothing], axis=1)
        summed = summed + jnp.concatenate([nothing, from_next], axis=1)
        results.append(mine * summed / views.shape[0])
    return jnp.concatenate(results, axis=0)


def solution(mesh):
    placed = (
        P(None, None, "bx", "by", None),
        P(None, "bx", "by", None),
        P("bx", "by", None, None, None),
        P(),
        P(),
    )
    return jax.shard_map(
        shards, mesh=mesh, in_specs=placed, out_specs=P(None, "bx", "by", None), check_vma=False
    )
```

```python
import functools

import jax
import jax.numpy as jnp
from jax import lax
from jax.experimental import pallas as pl
from jax.experimental.pallas import tpu as pltpu
from jax.sharding import PartitionSpec as P

F32 = jnp.float32
BF16 = jnp.bfloat16
SMALL = pltpu.CompilerParams(vmem_limit_bytes=8 * 1024 * 1024)
SKEW = 8
PAD = 16


def halves(value):
    high = value.astype(BF16)
    return high, (value - high.astype(F32)).astype(BF16)


def position(shape, dim, own, rim, reach, odd):
    at = lax.broadcasted_iota(jnp.int32, shape, dim)
    outside = 4 * own + 4 * rim
    step = jnp.where(at < own + rim, at - own, at - own - rim)
    above = own + step
    below = step - reach
    first = jnp.where(odd, below, above)
    second = jnp.where(odd, above, below)
    place = jnp.where(at < own + rim, first, second)
    place = jnp.where(step < reach, place, outside)
    return jnp.where(at < own, at, place)


def matrices(taps, parity, x_blur, x_back, y_blur, y_back, z_blur, z_back):
    views, _, count = taps.shape
    half = count // 2
    planes = x_blur.shape[0] // views
    wide = x_back.shape[0]
    width, slab = y_blur.shape[1], y_back.shape[1]
    depth = z_blur.shape[1] // 2
    odd_x, odd_y = parity[0] == 1, parity[1] == 1

    def pick(view, axis, offset):
        total = jnp.zeros(offset.shape, F32)
        for step in range(count):
            total = jnp.where(offset == step, taps[view, axis, step], total)
        return halves(total)

    def index(shape, dim):
        return lax.broadcasted_iota(jnp.int32, shape, dim)

    def tripled(high, low):
        return jnp.concatenate([high, high, low], axis=1)

    highs, lows = [], []
    for view in range(views):
        shape = (planes, wide)
        at = position(shape, 1, planes, PAD, half, odd_x)
        high, low = pick(view, 0, at - index(shape, 0) + half)
        x_blur[view * planes : (view + 1) * planes] = tripled(high, low)
        shape = (wide, planes)
        at = position(shape, 0, planes, PAD, half, odd_x)
        high, low = pick(view, 0, at - index(shape, 1) + half)
        highs.append(high)
        lows.append(low)
        shape = (width, slab)
        at = position(shape, 1, width, PAD, PAD, odd_y)
        y_blur[view] = tripled(*pick(view, 1, at - index(shape, 0) + half))
        shape = (slab, width)
        at = position(shape, 0, width, PAD, PAD, odd_y)
        y_back[view] = tripled(*pick(view, 1, at - index(shape, 1) + half))
        shape = (depth, depth)
        offset = index(shape, 0) - index(shape, 1) + half
        for ref, at in ((z_blur, offset), (z_back, 2 * half - offset)):
            high, low = pick(view, 2, at)
            ref[view, :depth] = jnp.concatenate([high, low], axis=1)
            ref[view, depth:] = jnp.concatenate([high, jnp.zeros_like(low)], axis=1)
    x_back[...] = jnp.concatenate(highs + highs + lows, axis=1)


def bands(kernels, parity, planes, width, depth):
    views = kernels.shape[0]
    wide, slab = planes + 2 * PAD, width + 2 * PAD
    shapes = [
        (views * planes, 3 * wide),
        (wide, 3 * views * planes),
        (views, width, 3 * slab),
        (views, slab, 3 * width),
        (views, 2 * depth, 2 * depth),
        (views, 2 * depth, 2 * depth),
    ]
    return pl.pallas_call(
        matrices,
        out_shape=[jax.ShapeDtypeStruct(s, BF16) for s in shapes],
        in_specs=[pl.BlockSpec(memory_space=pltpu.SMEM)] * 2,
        compiler_params=SMALL,
    )(kernels, parity)


def dot(left, right):
    return jnp.dot(left, right, preferred_element_type=F32)


def fused(
    own, xa, xb, yc, yd, views, lights, x_blur, x_back, y_blur, y_back, z_blur, z_back,
    s_own, s_xa, s_xb, s_yc, s_yd, ext, mid,
):
    count = views.shape[0]
    planes, width, depth = own.shape[1:]
    reach = xa.shape[1]
    wide, slab = planes + 2 * PAD, width + 2 * PAD
    pitch = slab + SKEW
    blocks = ((0, planes, own, s_own, 0), (planes, reach, xa, s_xa, planes), (planes + PAD, reach, xb, s_xb, planes + reach))

    def stacked(value):
        high, low = halves(value)
        return jnp.concatenate([high, low, high], axis=0)

    for start, size, ref, _, at in blocks:
        for i in range(size):
            base = (start + i) * pitch
            ext[base : base + width] = ref[0, i]
            ext[base + width : base + width + PAD] = yc[0, at + i]
            ext[base + width + PAD : base + slab] = yd[0, at + i]
    for plane in (planes + reach, planes + PAD + reach):
        ext[plane * pitch : plane * pitch + slab] = jnp.zeros((slab, depth), F32)

    rows = count * planes
    for y in range(0, slab, 2):
        pair = [stacked(ext[pl.ds(y + side, wide, stride=pitch), :]) for side in range(2)]
        out = dot(x_blur[...], jnp.concatenate(pair, axis=1))
        for side in range(2):
            mid[pl.ds(y + side, rows, stride=pitch), :] = out[:, side * depth : (side + 1) * depth]

    def through(value, matrix):
        high, low = halves(value)
        out = dot(jnp.concatenate([high, low], axis=1), matrix)
        return out[:, :depth] + out[:, depth:]

    def alone(view, matrix, values):
        outs = []
        for i in range(0, planes, 2):
            pair = jnp.concatenate([stacked(values[i]), stacked(values[i + 1])], axis=1)
            out = dot(matrix, pair)
            outs += [out[:, :depth], out[:, depth:]]
        return outs

    fields = []
    for view in range(count):
        bases = [(view * planes + i) * pitch for i in range(planes)]
        values = [mid[base : base + slab] for base in bases]
        fields.append(jnp.concatenate(alone(view, y_blur[view], values), axis=0))
    fields = [through(fields[view], z_blur[view]) for view in range(count)]
    ratios = []
    for view in range(count):
        light = lights[view][None]
        field = fields[view].reshape(planes, width, depth)
        ratio = light * views[view, 0] / (light * field + 0.05)
        ratios.append(ratio.reshape(planes * width, depth))
    backs = [through(ratios[view], z_back[view]) for view in range(count)]
    for view in range(count):
        values = [backs[view][i * width : (i + 1) * width] for i in range(planes)]
        for i, out in enumerate(alone(view, y_back[view], values)):
            base = (view * planes + i) * pitch
            mid[base : base + slab] = out

    for y in range(0, slab, 2):
        pair = [stacked(mid[pl.ds(y + side, rows, stride=pitch), :]) for side in range(2)]
        out = dot(x_back[...], jnp.concatenate(pair, axis=1))
        for side in range(2):
            ext[pl.ds(y + side, wide, stride=pitch), :] = out[:, side * depth : (side + 1) * depth]

    for start, size, _, ref, at in blocks:
        for i in range(size):
            base = (start + i) * pitch
            ref[0, i] = ext[base : base + width]
            s_yc[0, at + i] = ext[base + width : base + width + PAD]
            s_yd[0, at + i] = ext[base + width + PAD : base + slab]


def brick(channel, estimate, xa, xb, yc, yd, views, lights, mats):
    count = views.shape[0]
    planes, width, depth = estimate.shape[1:]
    reach = xa.shape[1]
    total = planes + 2 * reach
    wide, slab = planes + 2 * PAD, width + 2 * PAD

    shapes = [(1, planes, width, depth)] + [(1, reach, width, depth)] * 2 + [(1, total, PAD, depth)] * 2
    return pl.pallas_call(
        fused,
        grid=(1,),
        out_shape=[jax.ShapeDtypeStruct(s, F32) for s in shapes],
        in_specs=[
            pl.BlockSpec((1, planes, width, depth), lambda i: (channel, 0, 0, 0)),
            whole(xa), whole(xb), whole(yc), whole(yd),
            pl.BlockSpec((count, 1, planes, width, depth), lambda i: (0, channel, 0, 0, 0)),
            whole(lights),
        ] + [whole(m) for m in mats],
        out_specs=[pl.BlockSpec(s, lambda i: (0,) * 4) for s in shapes],
        scratch_shapes=[
            pltpu.VMEM((wide * (slab + SKEW), depth), F32),
            pltpu.VMEM((count * planes * (slab + SKEW), depth), F32),
        ],
        compiler_params=pltpu.CompilerParams(vmem_limit_bytes=24 * 1024 * 1024),
    )(estimate, xa, xb, yc, yd, views, lights, *mats)


def trade(value, axis, first):
    count = lax.axis_size(axis)
    pairs = []
    for low in range(0 if first else 1, count - 1, 2):
        pairs += [(low, low + 1), (low + 1, low)]
    return lax.ppermute(value, axis, pairs)


def illumination(profiles, owners, width):
    row, col = lax.axis_index("bx"), lax.axis_index("by")
    cols = lax.axis_size("by")
    source = lax.dynamic_index_in_dim(owners, row, axis=1, keepdims=False)
    count, _, depth = profiles.shape
    held = jnp.where((source == col)[:, None, None], profiles, F32(0.0))
    held = held.reshape(count, cols, width, depth)
    step = 1
    while step < cols:
        held = held.reshape(count, held.shape[1] // 2, 2, width, depth)
        odd = (col // step) % 2 == 1
        kept = jnp.where(odd, held[:, :, 1], held[:, :, 0])
        sent = jnp.where(odd, held[:, :, 0], held[:, :, 1])
        held = kept + lax.ppermute(sent, "by", [(i, i ^ step) for i in range(cols)])
        step *= 2
    return held.reshape(count, width, depth)


def whole(array):
    return pl.BlockSpec(array.shape, lambda i: (0,) * array.ndim)


SCALARS = pl.BlockSpec(memory_space=pltpu.SMEM)


def one_channel(array, channel):
    return pl.BlockSpec((1,) + array.shape[1:], lambda i: (channel, 0, 0, 0))


def row_starts(parity, width):
    first = jnp.where(parity[1] == 1, 0, width - PAD)
    second = jnp.where(parity[1] == 1, width - PAD, 0)
    return tuple(pl.ds(pl.multiple_of(start, PAD), PAD) for start in (first, second))


def rim_rows(parity, own, xa, xb, yc, yd):
    planes, width, reach = own.shape[1], own.shape[2], xa.shape[1]
    for out, rows in zip((yc, yd), row_starts(parity, width)):
        out[0, :planes] = own[0, :, rows, :]
        out[0, planes : planes + reach] = xa[0, :, rows, :]
        out[0, planes + reach :] = xb[0, :, rows, :]


def pack_rows(channel, parity, estimate, xa, xb):
    _, planes, _, depth = estimate.shape
    shape = (1, planes + 2 * xa.shape[1], PAD, depth)
    return pl.pallas_call(
        rim_rows,
        grid=(1,),
        out_shape=[jax.ShapeDtypeStruct(shape, F32)] * 2,
        in_specs=[SCALARS, one_channel(estimate, channel), whole(xa), whole(xb)],
        out_specs=[pl.BlockSpec(shape, lambda i: (0,) * 4)] * 2,
        compiler_params=SMALL,
    )(parity, estimate, xa, xb)


def rim_planes(parity, s_xa, s_xb, rc, rd, out_a, out_b):
    reach, width = s_xa.shape[1:3]
    base = rc.shape[1] - 2 * reach
    out_a[...] = s_xa[...]
    out_b[...] = s_xb[...]
    for got, rows in zip((rc, rd), row_starts(parity, width)):
        out_a[0, :, rows, :] += got[0, base : base + reach]
        out_b[0, :, rows, :] += got[0, base + reach :]


def pack_planes(parity, s_xa, s_xb, rc, rd):
    return pl.pallas_call(
        rim_planes,
        grid=(1,),
        out_shape=[jax.ShapeDtypeStruct(s_xa.shape, F32)] * 2,
        in_specs=[SCALARS, whole(s_xa), whole(s_xb), whole(rc), whole(rd)],
        out_specs=[whole(s_xa)] * 2,
        compiler_params=SMALL,
    )(parity, s_xa, s_xb, rc, rd)


def closing(parity, estimate, s_own, rc, rd, qa, qb, out, *, views):
    planes, width = s_own.shape[1:3]
    reach = qa.shape[1]
    out[...] = s_own[...]
    for got, rows in zip((rc, rd), row_starts(parity, width)):
        out[0, :, rows, :] += got[0, :planes]
    first = jnp.where(parity[0] == 1, 0, planes - reach)
    second = jnp.where(parity[0] == 1, planes - reach, 0)
    out[0, pl.ds(first, reach)] += qa[0]
    out[0, pl.ds(second, reach)] += qb[0]
    out[...] = estimate[...] * out[...] / views


def finish(channel, views, parity, estimate, s_own, rc, rd, qa, qb, done):
    planes = s_own.shape[1]

    def own_planes(array):
        return pl.BlockSpec((1, planes) + array.shape[2:], lambda i: (0,) * 4)

    def body(*refs):
        closing(*refs[:7], refs[-1], views=views)

    more = [] if done is None else [done]
    return pl.pallas_call(
        body,
        grid=(1,),
        out_shape=jax.ShapeDtypeStruct(estimate.shape, F32),
        in_specs=[
            SCALARS, one_channel(estimate, channel), whole(s_own), own_planes(rc), own_planes(rd),
            whole(qa), whole(qb),
        ] + [pl.BlockSpec(memory_space=pl.ANY)] * len(more),
        out_specs=one_channel(estimate, channel),
        compiler_params=SMALL,
        input_output_aliases={7: 0} if more else {},
    )(parity, estimate, s_own, rc, rd, qa, qb, *more)


def shards(views, estimate, profiles, kernels, owners):
    channels, planes, width, depth = estimate.shape
    reach = kernels.shape[2] // 2
    odd_x, odd_y = lax.axis_index("bx") % 2, lax.axis_index("by") % 2
    parity = jnp.stack([odd_x, odd_y]).astype(jnp.int32)
    x_first, x_second = (planes - reach) * (1 - odd_x), (planes - reach) * odd_x
    halo = []
    for c in range(channels):
        mine = estimate[c : c + 1]
        xa = trade(lax.dynamic_slice_in_dim(mine, x_first, reach, axis=1), "bx", True)
        xb = trade(lax.dynamic_slice_in_dim(mine, x_second, reach, axis=1), "bx", False)
        halo.append((xa, xb))
    mats = bands(kernels, parity, planes, width, depth)
    lights = illumination(profiles[0, 0], owners, width)
    parts = []
    for c in range(channels):
        xa, xb = halo[c]
        yc, yd = pack_rows(c, parity, estimate, xa, xb)
        yc, yd = trade(yc, "by", True), trade(yd, "by", False)
        parts.append(brick(c, estimate, xa, xb, yc, yd, views, lights, mats))
    ends = []
    for c in range(channels):
        s_own, s_xa, s_xb, s_yc, s_yd = parts[c]
        rc, rd = trade(s_yc, "by", True), trade(s_yd, "by", False)
        qa, qb = pack_planes(parity, s_xa, s_xb, rc, rd)
        ends.append((s_own, rc, rd, trade(qa, "bx", True), trade(qb, "bx", False)))
    done = None
    for c in range(channels):
        done = finish(c, views.shape[0], parity, estimate, *ends[c], done)
    return done


def solution(mesh):
    placed = (
        P(None, None, "bx", "by", None),
        P(None, "bx", "by", None),
        P("bx", "by", None, None, None),
        P(),
        P(),
    )
    return jax.shard_map(
        shards, mesh=mesh, in_specs=placed, out_specs=P(None, "bx", "by", None), check_vma=False
    )
```

```python
import functools

import jax
import jax.numpy as jnp
from jax import lax
from jax.experimental import pallas as pl
from jax.experimental.pallas import tpu as pltpu
from jax.sharding import PartitionSpec as P

F32 = jnp.float32
BF16 = jnp.bfloat16
SMALL = pltpu.CompilerParams(vmem_limit_bytes=8 * 1024 * 1024)
FREE = pl.CostEstimate(flops=0, bytes_accessed=0, transcendentals=0)
SKEW = 8
PAD = 16


def halves(value):
    high = value.astype(BF16)
    return high, (value - high.astype(F32)).astype(BF16)


def position(shape, dim, own, rim, reach, odd):
    at = lax.broadcasted_iota(jnp.int32, shape, dim)
    outside = 4 * own + 4 * rim
    step = jnp.where(at < own + rim, at - own, at - own - rim)
    above = own + step
    below = step - reach
    first = jnp.where(odd, below, above)
    second = jnp.where(odd, above, below)
    place = jnp.where(at < own + rim, first, second)
    place = jnp.where(step < reach, place, outside)
    return jnp.where(at < own, at, place)


def matrices(taps, parity, _, x_blur, x_back, y_blur, y_back, z_blur, z_back):
    views, _, count = taps.shape
    half = count // 2
    planes = x_blur.shape[0] // views
    wide = x_back.shape[0]
    width, slab = y_blur.shape[1], y_back.shape[1]
    depth = z_blur.shape[1] // 2
    odd_x, odd_y = parity[0] % 2 == 1, parity[1] % 2 == 1

    def pick(view, axis, offset):
        total = jnp.zeros(offset.shape, F32)
        for step in range(count):
            total = jnp.where(offset == step, taps[view, axis, step], total)
        return halves(total)

    def index(shape, dim):
        return lax.broadcasted_iota(jnp.int32, shape, dim)

    def tripled(high, low):
        return jnp.concatenate([high, high, low], axis=1)

    highs, lows = [], []
    for view in range(views):
        shape = (planes, wide)
        at = position(shape, 1, planes, PAD, half, odd_x)
        high, low = pick(view, 0, at - index(shape, 0) + half)
        x_blur[view * planes : (view + 1) * planes] = tripled(high, low)
        shape = (wide, planes)
        at = position(shape, 0, planes, PAD, half, odd_x)
        high, low = pick(view, 0, at - index(shape, 1) + half)
        highs.append(high)
        lows.append(low)
        shape = (width, slab)
        at = position(shape, 1, width, PAD, PAD, odd_y)
        y_blur[view] = tripled(*pick(view, 1, at - index(shape, 0) + half))
        shape = (slab, width)
        at = position(shape, 0, width, PAD, PAD, odd_y)
        y_back[view] = tripled(*pick(view, 1, at - index(shape, 1) + half))
        shape = (depth, depth)
        offset = index(shape, 0) - index(shape, 1) + half
        for ref, at in ((z_blur, offset), (z_back, 2 * half - offset)):
            high, low = pick(view, 2, at)
            ref[view, :depth] = jnp.concatenate([high, low], axis=1)
            ref[view, depth:] = jnp.concatenate([high, jnp.zeros_like(low)], axis=1)
    x_back[...] = jnp.concatenate(highs + highs + lows, axis=1)


def bands(kernels, parity, planes, width, depth, after):
    views = kernels.shape[0]
    wide, slab = planes + 2 * PAD, width + 2 * PAD
    shapes = [
        (views * planes, 3 * wide),
        (wide, 3 * views * planes),
        (views, width, 3 * slab),
        (views, slab, 3 * width),
        (views, 2 * depth, 2 * depth),
        (views, 2 * depth, 2 * depth),
    ]
    return pl.pallas_call(
        matrices,
        out_shape=[jax.ShapeDtypeStruct(s, BF16) for s in shapes],
        in_specs=[pl.BlockSpec(memory_space=pltpu.SMEM)] * 2 + [LATER],
        compiler_params=SMALL,
        name="matrices",
    )(kernels, parity, after)


def dot(left, right):
    return jnp.dot(left, right, preferred_element_type=F32)


def fused(
    own, xa, xb, yc, yd, views, light_kept, light_got, x_blur, x_back, y_blur, y_back, z_blur, z_back, _,
    s_own, s_xa, s_xb, s_yc, s_yd, ext, mid,
):
    count = views.shape[0]
    planes, width, depth = own.shape[1:]
    reach = xa.shape[1]
    wide, slab = planes + 2 * PAD, width + 2 * PAD
    pitch = slab + SKEW
    blocks = ((0, planes, own, s_own, 0), (planes, reach, xa, s_xa, planes), (planes + PAD, reach, xb, s_xb, planes + reach))

    def stacked(value):
        high, low = halves(value)
        return jnp.concatenate([high, low, high], axis=0)

    for start, size, ref, _, at in blocks:
        for i in range(size):
            base = (start + i) * pitch
            ext[base : base + width] = ref[0, i]
            ext[base + width : base + width + PAD] = yc[0, at + i]
            ext[base + width + PAD : base + slab] = yd[0, at + i]
    for plane in (planes + reach, planes + PAD + reach):
        ext[plane * pitch : plane * pitch + slab] = jnp.zeros((slab, depth), F32)

    rows = count * planes
    for y in range(0, slab, 2):
        pair = [stacked(ext[pl.ds(y + side, wide, stride=pitch), :]) for side in range(2)]
        out = dot(x_blur[...], jnp.concatenate(pair, axis=1))
        for side in range(2):
            mid[pl.ds(y + side, rows, stride=pitch), :] = out[:, side * depth : (side + 1) * depth]

    def through(value, matrix):
        high, low = halves(value)
        out = dot(jnp.concatenate([high, low], axis=1), matrix)
        return out[:, :depth] + out[:, depth:]

    def alone(view, matrix, values):
        outs = []
        for i in range(0, planes, 2):
            pair = jnp.concatenate([stacked(values[i]), stacked(values[i + 1])], axis=1)
            out = dot(matrix, pair)
            outs += [out[:, :depth], out[:, depth:]]
        return outs

    fields = []
    for view in range(count):
        bases = [(view * planes + i) * pitch for i in range(planes)]
        values = [mid[base : base + slab] for base in bases]
        fields.append(jnp.concatenate(alone(view, y_blur[view], values), axis=0))
    fields = [through(fields[view], z_blur[view]) for view in range(count)]
    ratios = []
    for view in range(count):
        light = (light_kept[view] + light_got[view])[None]
        field = fields[view].reshape(planes, width, depth)
        ratio = light * views[view, 0] / (light * field + 0.05)
        ratios.append(ratio.reshape(planes * width, depth))
    backs = [through(ratios[view], z_back[view]) for view in range(count)]
    for view in range(count):
        values = [backs[view][i * width : (i + 1) * width] for i in range(planes)]
        for i, out in enumerate(alone(view, y_back[view], values)):
            base = (view * planes + i) * pitch
            mid[base : base + slab] = out

    for y in range(0, slab, 2):
        pair = [stacked(mid[pl.ds(y + side, rows, stride=pitch), :]) for side in range(2)]
        out = dot(x_back[...], jnp.concatenate(pair, axis=1))
        for side in range(2):
            ext[pl.ds(y + side, wide, stride=pitch), :] = out[:, side * depth : (side + 1) * depth]

    for start, size, _, ref, at in blocks:
        for i in range(size):
            base = (start + i) * pitch
            ref[0, i] = ext[base : base + width]
            s_yc[0, at + i] = ext[base + width : base + width + PAD]
            s_yd[0, at + i] = ext[base + width + PAD : base + slab]


def brick(channel, estimate, xa, xb, yc, yd, views, lights, mats, after):
    count = views.shape[0]
    planes, width, depth = estimate.shape[1:]
    reach = xa.shape[1]
    total = planes + 2 * reach
    wide, slab = planes + 2 * PAD, width + 2 * PAD

    shapes = [(1, planes, width, depth)] + [(1, reach, width, depth)] * 2 + [(1, total, PAD, depth)] * 2
    return pl.pallas_call(
        fused,
        grid=(1,),
        out_shape=[jax.ShapeDtypeStruct(s, F32) for s in shapes],
        in_specs=[
            pl.BlockSpec((1, planes, width, depth), lambda i: (channel, 0, 0, 0)),
            whole(xa), whole(xb), whole(yc), whole(yd),
            pl.BlockSpec((count, 1, planes, width, depth), lambda i: (0, channel, 0, 0, 0)),
        ] + [whole(m) for m in (*lights, *mats)] + [LATER],
        out_specs=[pl.BlockSpec(s, lambda i: (0,) * 4) for s in shapes],
        scratch_shapes=[
            pltpu.VMEM((wide * (slab + SKEW), depth), F32),
            pltpu.VMEM((count * planes * (slab + SKEW), depth), F32),
        ],
        compiler_params=pltpu.CompilerParams(vmem_limit_bytes=24 * 1024 * 1024),
        name="brick%d" % channel,
    )(estimate, xa, xb, yc, yd, views, *lights, *mats, after)


def trade(value, axis, first):
    count = lax.axis_size(axis)
    pairs = []
    for low in range(0 if first else 1, count - 1, 2):
        pairs += [(low, low + 1), (low + 1, low)]
    return lax.ppermute(value, axis, pairs)


def whole(array):
    return pl.BlockSpec(array.shape, lambda i: (0,) * len(array.shape))


SCALARS = pl.BlockSpec(memory_space=pltpu.SMEM)
LATER = pl.BlockSpec(memory_space=pl.ANY)


def one_channel(array, channel):
    return pl.BlockSpec((1,) + array.shape[1:], lambda i: (channel, 0, 0, 0))


def call(body, name, ins, outs, deps=(), **more):
    count = len(ins)

    def kernel(*refs):
        body(*refs[:count], *refs[count + len(deps) :])

    out = pl.pallas_call(
        kernel,
        grid=(1,),
        out_shape=[jax.ShapeDtypeStruct(s, F32) for s in outs],
        in_specs=[spec for spec, _ in ins] + [LATER] * len(deps),
        out_specs=[pl.BlockSpec(s, lambda i, n=len(s): (0,) * n) for s in outs],
        compiler_params=SMALL,
        name=name,
        **more,
    )
    return out(*[array for _, array in ins], *deps)


def mask_profiles(cols, place, owners, profile, estimate, deps):
    _, _, count, _, depth = profile.shape
    width = estimate.shape[2]
    shape = (count, cols // 2, width, depth)

    def body(place, owners, profile, kept, sent):
        bit = place[1] % 2
        for view in range(count):
            valid = owners[view, place[0]] == place[1]
            for block in range(cols // 2):
                for ref, side in ((kept, bit), (sent, 1 - bit)):
                    start = pl.multiple_of((2 * block + side) * width, width)
                    value = profile[0, 0, view, pl.ds(start, width), :]
                    ref[view, block] = jnp.where(valid, value, 0.0)

    return call(
        body, "mask_profiles",
        [(SCALARS, place), (SCALARS, owners), (whole(profile), profile)], [shape] * 2, deps,
    )


def halve_profiles(step, place, kept, got, deps):
    count, blocks, width, depth = kept.shape
    shape = (count, blocks // 2, width, depth)

    def body(place, kept, got, out_kept, out_sent):
        bit = place[1] // step % 2
        for view in range(count):
            for block in range(blocks // 2):
                for ref, side in ((out_kept, bit), (out_sent, 1 - bit)):
                    at = 2 * block + side
                    ref[view, block] = kept[view, at] + got[view, at]

    return call(
        body, "halve_profiles%d" % step,
        [(SCALARS, place), (whole(kept), kept), (whole(got), got)], [shape] * 2, deps,
    )


def pack_planes(place, estimate, reach):
    channels, planes, width, depth = estimate.shape

    def body(place, own, *outs):
        odd = place[0] % 2
        for channel in range(channels):
            for out, side in zip(outs[2 * channel :], (1 - odd, odd)):
                out[0] = own[channel, pl.ds((planes - reach) * side, reach)]

    return call(
        body, "pack_planes", [(SCALARS, place), (whole(estimate), estimate)],
        [(1, reach, width, depth)] * (2 * channels),
    )


def row_starts(place, width):
    odd = place[1] % 2
    starts = ((width - PAD) * (1 - odd), (width - PAD) * odd)
    return tuple(pl.ds(pl.multiple_of(start, PAD), PAD) for start in starts)


def pack_rows(channel, place, estimate, xa, xb, deps):
    _, planes, width, depth = estimate.shape
    reach = xa.shape[1]

    def body(place, own, xa, xb, first, second):
        for out, rows in zip((first, second), row_starts(place, width)):
            out[0, :planes] = own[0, :, rows, :]
            out[0, planes : planes + reach] = xa[0, :, rows, :]
            out[0, planes + reach :] = xb[0, :, rows, :]

    return call(
        body, "pack_rows%d" % channel,
        [(SCALARS, place), (one_channel(estimate, channel), estimate), (whole(xa), xa), (whole(xb), xb)],
        [(1, planes + 2 * reach, PAD, depth)] * 2, deps,
    )


def add_rows(channel, place, s_xa, s_xb, rc, rd, deps):
    reach, width = s_xa.shape[1:3]
    base = rc.shape[1] - 2 * reach

    def body(place, s_xa, s_xb, rc, rd, first, second):
        first[...] = s_xa[...]
        second[...] = s_xb[...]
        for got, rows in zip((rc, rd), row_starts(place, width)):
            first[0, :, rows, :] += got[0, base : base + reach]
            second[0, :, rows, :] += got[0, base + reach :]

    return call(
        body, "add_rows%d" % channel,
        [(SCALARS, place)] + [(whole(a), a) for a in (s_xa, s_xb, rc, rd)], [s_xa.shape] * 2, deps,
    )


def finish(channel, views, place, estimate, s_own, rc, rd, qa, qb, done, deps):
    planes, width = s_own.shape[1:3]
    reach = qa.shape[1]

    def own_planes(array):
        return pl.BlockSpec((1, planes) + array.shape[2:], lambda i: (0,) * 4)

    def body(place, estimate, s_own, rc, rd, qa, qb, *rest):
        out = rest[-1]
        out[...] = s_own[...]
        for got, rows in zip((rc, rd), row_starts(place, width)):
            out[0, :, rows, :] += got[0]
        odd = place[0] % 2
        out[0, pl.ds((planes - reach) * (1 - odd), reach)] += qa[0]
        out[0, pl.ds((planes - reach) * odd, reach)] += qb[0]
        out[...] = estimate[...] * out[...] / views

    more = [] if done is None else [done]
    ins = [place, estimate, s_own, rc, rd, qa, qb] + more + list(deps)
    return pl.pallas_call(
        body,
        grid=(1,),
        out_shape=jax.ShapeDtypeStruct(estimate.shape, F32),
        in_specs=[
            SCALARS, one_channel(estimate, channel), whole(s_own), own_planes(rc), own_planes(rd),
            whole(qa), whole(qb),
        ] + [LATER] * (len(more) + len(deps)),
        out_specs=one_channel(estimate, channel),
        input_output_aliases={7: 0} if more else {},
        compiler_params=SMALL,
        name="finish%d" % channel,
    )(*ins)


def flip(value, axis, step):
    return lax.ppermute(value, axis, [(i, i ^ step) for i in range(lax.axis_size(axis))])


def shards(views, estimate, profiles, kernels, owners):
    channels, planes, width, depth = estimate.shape
    reach = kernels.shape[2] // 2
    cols = lax.axis_size("by")
    place = jnp.stack([lax.axis_index("bx"), lax.axis_index("by")]).astype(jnp.int32)
    odd = place[0] % 2
    packed = []
    for c in range(channels):
        for side in (1 - odd, odd):
            packed.append(lax.dynamic_slice_in_dim(estimate[c : c + 1], (planes - reach) * side, reach, axis=1))
    halo = []
    for c in range(channels):
        xb = trade(packed[2 * c + 1], "bx", False)
        halo.append((trade(packed[2 * c], "bx", True), xb))
    kept, sent = mask_profiles(cols, place, owners, profiles, estimate, (packed[0],))
    step, mats = 1, None
    while True:
        got = flip(sent, "by", step)
        if mats is None:
            mats = bands(kernels, place, planes, width, depth, sent)
        step *= 2
        if step == cols:
            break
        kept, sent = halve_profiles(step, place, kept, got, (mats[0],))
    lights = (kept.reshape(-1, width, depth), got.reshape(-1, width, depth))
    rims = []
    for c in range(channels):
        xa, xb = halo[c]
        yc, yd = pack_rows(c, place, estimate, xa, xb, (got,))
        yd = trade(yd, "by", False)
        rims.append((yc, trade(yc, "by", True), yd))
    ends, sums, done, prev = [], kernels, None, ()
    for c in range(channels):
        _, yc, yd = rims[c]
        s_own, s_xa, s_xb, s_yc, s_yd = brick(c, estimate, *halo[c], yc, yd, views, lights, mats, sums)
        rd = trade(s_yd, "by", False)
        rc = trade(s_yc, "by", True)
        first, second = add_rows(c, place, s_xa, s_xb, rc, rd, prev)
        sums = kernels
        qb = trade(second, "bx", False)
        qa = trade(first, "bx", True)
        prev = ()
        ends.append((s_own, rc, rd, qa, qb))
    done = None
    for c in range(channels):
        done = finish(c, views.shape[0], place, estimate, *ends[c], done, (sums,))
    return done


def solution(mesh):
    placed = (
        P(None, None, "bx", "by", None),
        P(None, "bx", "by", None),
        P("bx", "by", None, None, None),
        P(),
        P(),
    )
    return jax.shard_map(
        shards, mesh=mesh, in_specs=placed, out_specs=P(None, "bx", "by", None), check_vma=False
    )
```

```python
import functools

import jax
import jax.numpy as jnp
from jax import lax
from jax.experimental import pallas as pl
from jax.experimental.pallas import tpu as pltpu
from jax.sharding import PartitionSpec as P

F32 = jnp.float32
BF16 = jnp.bfloat16
SMALL = pltpu.CompilerParams(vmem_limit_bytes=8 * 1024 * 1024)
FREE = pl.CostEstimate(flops=0, bytes_accessed=0, transcendentals=0)
SKEW = 8
PAD = 16


def halves(value):
    high = value.astype(BF16)
    return high, (value - high.astype(F32)).astype(BF16)


def position(shape, dim, own, rim, reach, odd):
    at = lax.broadcasted_iota(jnp.int32, shape, dim)
    outside = 4 * own + 4 * rim
    step = jnp.where(at < own + rim, at - own, at - own - rim)
    above = own + step
    below = step - reach
    first = jnp.where(odd, below, above)
    second = jnp.where(odd, above, below)
    place = jnp.where(at < own + rim, first, second)
    place = jnp.where(step < reach, place, outside)
    return jnp.where(at < own, at, place)


def matrices(taps, parity, _, x_blur, x_back, y_blur, y_back, z_blur, z_back):
    views, _, count = taps.shape
    half = count // 2
    planes = x_blur.shape[0] // views
    wide = x_back.shape[0]
    width, slab = y_blur.shape[1], y_back.shape[1]
    depth = z_blur.shape[1] // 2
    odd_x, odd_y = parity[0] % 2 == 1, parity[1] % 2 == 1

    def pick(view, axis, offset):
        total = jnp.zeros(offset.shape, F32)
        for step in range(count):
            total = jnp.where(offset == step, taps[view, axis, step], total)
        return halves(total)

    def index(shape, dim):
        return lax.broadcasted_iota(jnp.int32, shape, dim)

    def tripled(high, low):
        return jnp.concatenate([high, high, low], axis=1)

    highs, lows = [], []
    for view in range(views):
        shape = (planes, wide)
        at = position(shape, 1, planes, PAD, half, odd_x)
        high, low = pick(view, 0, at - index(shape, 0) + half)
        x_blur[view * planes : (view + 1) * planes] = tripled(high, low)
        shape = (wide, planes)
        at = position(shape, 0, planes, PAD, half, odd_x)
        high, low = pick(view, 0, at - index(shape, 1) + half)
        highs.append(high)
        lows.append(low)
        shape = (width, slab)
        at = position(shape, 1, width, PAD, PAD, odd_y)
        y_blur[view] = tripled(*pick(view, 1, at - index(shape, 0) + half))
        shape = (slab, width)
        at = position(shape, 0, width, PAD, PAD, odd_y)
        y_back[view] = tripled(*pick(view, 1, at - index(shape, 1) + half))
        shape = (depth, depth)
        offset = index(shape, 0) - index(shape, 1) + half
        for ref, at in ((z_blur, offset), (z_back, 2 * half - offset)):
            high, low = pick(view, 2, at)
            ref[view, :depth] = jnp.concatenate([high, low], axis=1)
            ref[view, depth:] = jnp.concatenate([high, jnp.zeros_like(low)], axis=1)
    x_back[...] = jnp.concatenate(highs + highs + lows, axis=1)


def bands(kernels, parity, planes, width, depth, after):
    views = kernels.shape[0]
    wide, slab = planes + 2 * PAD, width + 2 * PAD
    shapes = [
        (views * planes, 3 * wide),
        (wide, 3 * views * planes),
        (views, width, 3 * slab),
        (views, slab, 3 * width),
        (views, 2 * depth, 2 * depth),
        (views, 2 * depth, 2 * depth),
    ]
    return pl.pallas_call(
        matrices,
        out_shape=[jax.ShapeDtypeStruct(s, BF16) for s in shapes],
        in_specs=[pl.BlockSpec(memory_space=pltpu.SMEM)] * 2 + [LATER],
        compiler_params=SMALL,
        name="matrices",
    )(kernels, parity, after)


def dot(left, right):
    return jnp.dot(left, right, preferred_element_type=F32)


def fused(
    own, xa, xb, yc, yd, views, light_kept, light_got, x_blur, x_back, y_blur, y_back, z_blur, z_back, _,
    s_own, s_xa, s_xb, s_yc, s_yd, ext, mid,
):
    count = views.shape[0]
    planes, width, depth = own.shape[1:]
    reach = xa.shape[1]
    wide, slab = planes + 2 * PAD, width + 2 * PAD
    pitch = slab + SKEW
    blocks = ((0, planes, own, s_own, 0), (planes, reach, xa, s_xa, planes), (planes + PAD, reach, xb, s_xb, planes + reach))

    def stacked(value):
        high, low = halves(value)
        return jnp.concatenate([high, low, high], axis=0)

    for start, size, ref, _, at in blocks:
        for i in range(size):
            base = (start + i) * pitch
            ext[base : base + width] = ref[0, i]
            ext[base + width : base + width + PAD] = yc[0, at + i]
            ext[base + width + PAD : base + slab] = yd[0, at + i]
    for plane in (planes + reach, planes + PAD + reach):
        ext[plane * pitch : plane * pitch + slab] = jnp.zeros((slab, depth), F32)

    rows = count * planes
    for y in range(0, slab, 2):
        pair = [stacked(ext[pl.ds(y + side, wide, stride=pitch), :]) for side in range(2)]
        out = dot(x_blur[...], jnp.concatenate(pair, axis=1))
        for side in range(2):
            mid[pl.ds(y + side, rows, stride=pitch), :] = out[:, side * depth : (side + 1) * depth]

    def through(value, matrix):
        high, low = halves(value)
        out = dot(jnp.concatenate([high, low], axis=1), matrix)
        return out[:, :depth] + out[:, depth:]

    def alone(view, matrix, values):
        outs = []
        for i in range(0, planes, 2):
            pair = jnp.concatenate([stacked(values[i]), stacked(values[i + 1])], axis=1)
            out = dot(matrix, pair)
            outs += [out[:, :depth], out[:, depth:]]
        return outs

    fields = []
    for view in range(count):
        bases = [(view * planes + i) * pitch for i in range(planes)]
        values = [mid[base : base + slab] for base in bases]
        fields.append(jnp.concatenate(alone(view, y_blur[view], values), axis=0))
    fields = [through(fields[view], z_blur[view]) for view in range(count)]
    ratios = []
    for view in range(count):
        light = (light_kept[view] + light_got[view])[None]
        field = fields[view].reshape(planes, width, depth)
        ratio = light * views[view, 0] / (light * field + 0.05)
        ratios.append(ratio.reshape(planes * width, depth))
    backs = [through(ratios[view], z_back[view]) for view in range(count)]
    for view in range(count):
        values = [backs[view][i * width : (i + 1) * width] for i in range(planes)]
        for i, out in enumerate(alone(view, y_back[view], values)):
            base = (view * planes + i) * pitch
            mid[base : base + slab] = out

    for y in range(0, slab, 2):
        pair = [stacked(mid[pl.ds(y + side, rows, stride=pitch), :]) for side in range(2)]
        out = dot(x_back[...], jnp.concatenate(pair, axis=1))
        for side in range(2):
            ext[pl.ds(y + side, wide, stride=pitch), :] = out[:, side * depth : (side + 1) * depth]

    for start, size, _, ref, at in blocks:
        for i in range(size):
            base = (start + i) * pitch
            ref[0, i] = ext[base : base + width]
            s_yc[0, at + i] = ext[base + width : base + width + PAD]
            s_yd[0, at + i] = ext[base + width + PAD : base + slab]


def brick(channel, estimate, xa, xb, yc, yd, views, lights, mats, after):
    count = views.shape[0]
    planes, width, depth = estimate.shape[1:]
    reach = xa.shape[1]
    total = planes + 2 * reach
    wide, slab = planes + 2 * PAD, width + 2 * PAD

    shapes = [(1, planes, width, depth)] + [(1, reach, width, depth)] * 2 + [(1, total, PAD, depth)] * 2
    return pl.pallas_call(
        fused,
        grid=(1,),
        out_shape=[jax.ShapeDtypeStruct(s, F32) for s in shapes],
        in_specs=[
            pl.BlockSpec((1, planes, width, depth), lambda i: (channel, 0, 0, 0)),
            whole(xa), whole(xb), whole(yc), whole(yd),
            pl.BlockSpec((count, 1, planes, width, depth), lambda i: (0, channel, 0, 0, 0)),
        ] + [whole(m) for m in (*lights, *mats)] + [LATER],
        out_specs=[pl.BlockSpec(s, lambda i: (0,) * 4) for s in shapes],
        scratch_shapes=[
            pltpu.VMEM((wide * (slab + SKEW), depth), F32),
            pltpu.VMEM((count * planes * (slab + SKEW), depth), F32),
        ],
        compiler_params=pltpu.CompilerParams(vmem_limit_bytes=24 * 1024 * 1024),
        name="brick%d" % channel,
    )(estimate, xa, xb, yc, yd, views, *lights, *mats, after)


def trade(value, axis, first):
    count = lax.axis_size(axis)
    pairs = []
    for low in range(0 if first else 1, count - 1, 2):
        pairs += [(low, low + 1), (low + 1, low)]
    return lax.ppermute(value, axis, pairs)


def whole(array):
    return pl.BlockSpec(array.shape, lambda i: (0,) * len(array.shape))


SCALARS = pl.BlockSpec(memory_space=pltpu.SMEM)
LATER = pl.BlockSpec(memory_space=pl.ANY)


def one_channel(array, channel):
    return pl.BlockSpec((1,) + array.shape[1:], lambda i: (channel, 0, 0, 0))


def call(body, name, ins, outs, deps=(), **more):
    count = len(ins)

    def kernel(*refs):
        body(*refs[:count], *refs[count + len(deps) :])

    out = pl.pallas_call(
        kernel,
        grid=(1,),
        out_shape=[jax.ShapeDtypeStruct(s, F32) for s in outs],
        in_specs=[spec for spec, _ in ins] + [LATER] * len(deps),
        out_specs=[pl.BlockSpec(s, lambda i, n=len(s): (0,) * n) for s in outs],
        compiler_params=SMALL,
        name=name,
        **more,
    )
    return out(*[array for _, array in ins], *deps)


def mask_profiles(cols, place, owners, profile, estimate, deps):
    _, _, count, _, depth = profile.shape
    width = estimate.shape[2]
    shape = (count, cols // 2, width, depth)

    def body(place, owners, profile, kept, sent):
        bit = place[1] % 2
        for view in range(count):
            valid = owners[view, place[0]] == place[1]
            for block in range(cols // 2):
                for ref, side in ((kept, bit), (sent, 1 - bit)):
                    start = pl.multiple_of((2 * block + side) * width, width)
                    value = profile[0, 0, view, pl.ds(start, width), :]
                    ref[view, block] = jnp.where(valid, value, 0.0)

    return call(
        body, "mask_profiles",
        [(SCALARS, place), (SCALARS, owners), (whole(profile), profile)], [shape] * 2, deps,
    )


def halve_profiles(step, place, kept, got, deps):
    count, blocks, width, depth = kept.shape
    shape = (count, blocks // 2, width, depth)

    def body(place, kept, got, out_kept, out_sent):
        bit = place[1] // step % 2
        for view in range(count):
            for block in range(blocks // 2):
                for ref, side in ((out_kept, bit), (out_sent, 1 - bit)):
                    at = 2 * block + side
                    ref[view, block] = kept[view, at] + got[view, at]

    return call(
        body, "halve_profiles%d" % step,
        [(SCALARS, place), (whole(kept), kept), (whole(got), got)], [shape] * 2, deps,
    )


def pack_planes(place, estimate, reach):
    channels, planes, width, depth = estimate.shape

    def body(place, own, *outs):
        odd = place[0] % 2
        for channel in range(channels):
            for out, side in zip(outs[2 * channel :], (1 - odd, odd)):
                out[0] = own[channel, pl.ds((planes - reach) * side, reach)]

    return call(
        body, "pack_planes", [(SCALARS, place), (whole(estimate), estimate)],
        [(1, reach, width, depth)] * (2 * channels),
    )


def row_starts(place, width):
    odd = place[1] % 2
    starts = ((width - PAD) * (1 - odd), (width - PAD) * odd)
    return tuple(pl.ds(pl.multiple_of(start, PAD), PAD) for start in starts)


def pack_rows(channel, place, estimate, xa, xb, deps):
    _, planes, width, depth = estimate.shape
    reach = xa.shape[1]

    def body(place, own, xa, xb, first, second):
        for out, rows in zip((first, second), row_starts(place, width)):
            out[0, :planes] = own[0, :, rows, :]
            out[0, planes : planes + reach] = xa[0, :, rows, :]
            out[0, planes + reach :] = xb[0, :, rows, :]

    return call(
        body, "pack_rows%d" % channel,
        [(SCALARS, place), (one_channel(estimate, channel), estimate), (whole(xa), xa), (whole(xb), xb)],
        [(1, planes + 2 * reach, PAD, depth)] * 2, deps,
    )


def add_rows(channel, place, s_xa, s_xb, rc, rd, deps):
    reach, width = s_xa.shape[1:3]
    base = rc.shape[1] - 2 * reach

    def body(place, s_xa, s_xb, rc, rd, first, second):
        first[...] = s_xa[...]
        second[...] = s_xb[...]
        for got, rows in zip((rc, rd), row_starts(place, width)):
            first[0, :, rows, :] += got[0, base : base + reach]
            second[0, :, rows, :] += got[0, base + reach :]

    return call(
        body, "add_rows%d" % channel,
        [(SCALARS, place)] + [(whole(a), a) for a in (s_xa, s_xb, rc, rd)], [s_xa.shape] * 2, deps,
    )


def finish(channel, views, place, estimate, s_own, rc, rd, qa, qb, done, deps):
    planes, width = s_own.shape[1:3]
    reach = qa.shape[1]

    def own_planes(array):
        return pl.BlockSpec((1, planes) + array.shape[2:], lambda i: (0,) * 4)

    def body(place, estimate, s_own, rc, rd, qa, qb, *rest):
        out = rest[-1]
        out[...] = s_own[...]
        for got, rows in zip((rc, rd), row_starts(place, width)):
            out[0, :, rows, :] += got[0]
        odd = place[0] % 2
        out[0, pl.ds((planes - reach) * (1 - odd), reach)] += qa[0]
        out[0, pl.ds((planes - reach) * odd, reach)] += qb[0]
        out[...] = estimate[...] * out[...] / views

    more = [] if done is None else [done]
    ins = [place, estimate, s_own, rc, rd, qa, qb] + more + list(deps)
    return pl.pallas_call(
        body,
        grid=(1,),
        out_shape=jax.ShapeDtypeStruct(estimate.shape, F32),
        in_specs=[
            SCALARS, one_channel(estimate, channel), whole(s_own), own_planes(rc), own_planes(rd),
            whole(qa), whole(qb),
        ] + [LATER] * (len(more) + len(deps)),
        out_specs=one_channel(estimate, channel),
        input_output_aliases={7: 0} if more else {},
        compiler_params=SMALL,
        name="finish%d" % channel,
    )(*ins)


def flip(value, axis, step):
    return lax.ppermute(value, axis, [(i, i ^ step) for i in range(lax.axis_size(axis))])


def shards(views, estimate, profiles, kernels, owners):
    channels, planes, width, depth = estimate.shape
    reach = kernels.shape[2] // 2
    cols = lax.axis_size("by")
    place = jnp.stack([lax.axis_index("bx"), lax.axis_index("by")]).astype(jnp.int32)
    odd = place[0] % 2
    packed = []
    for c in range(channels):
        for side in (1 - odd, odd):
            packed.append(lax.dynamic_slice_in_dim(estimate[c : c + 1], (planes - reach) * side, reach, axis=1))
    halo = []
    for c in range(channels):
        xb = trade(packed[2 * c + 1], "bx", False)
        halo.append((trade(packed[2 * c], "bx", True), xb))
    kept, sent = mask_profiles(cols, place, owners, profiles, estimate, (packed[0],))
    step, mats = 1, None
    while True:
        got = flip(sent, "by", step)
        step *= 2
        if step == cols:
            break
        kept, sent = halve_profiles(step, place, kept, got, () if mats is None else (mats[0],))
        if mats is None:
            mats = bands(kernels, place, planes, width, depth, sent)
    if mats is None:
        mats = bands(kernels, place, planes, width, depth, sent)
    lights = (kept.reshape(-1, width, depth), got.reshape(-1, width, depth))
    rims = []
    for c in range(channels):
        xa, xb = halo[c]
        yc, yd = pack_rows(c, place, estimate, xa, xb, (sent if c == 0 else got,))
        yd = trade(yd, "by", False)
        rims.append((yc, trade(yc, "by", True), yd))
    ends, sums, done, prev = [], kernels, None, ()
    for c in range(channels):
        _, yc, yd = rims[c]
        s_own, s_xa, s_xb, s_yc, s_yd = brick(c, estimate, *halo[c], yc, yd, views, lights, mats, sums)
        rd = trade(s_yd, "by", False)
        rc = trade(s_yc, "by", True)
        first, second = add_rows(c, place, s_xa, s_xb, rc, rd, prev)
        sums = kernels
        qb = trade(second, "bx", False)
        qa = trade(first, "bx", True)
        prev = ()
        ends.append((s_own, rc, rd, qa, qb))
    done = None
    for c in range(channels):
        done = finish(c, views.shape[0], place, estimate, *ends[c], done, (sums,))
    return done


def solution(mesh):
    placed = (
        P(None, None, "bx", "by", None),
        P(None, "bx", "by", None),
        P("bx", "by", None, None, None),
        P(),
        P(),
    )
    return jax.shard_map(
        shards, mesh=mesh, in_specs=placed, out_specs=P(None, "bx", "by", None), check_vma=False
    )
```

```python
import functools

import jax
import jax.numpy as jnp
from jax import lax
from jax.experimental import pallas as pl
from jax.experimental.pallas import tpu as pltpu
from jax.sharding import PartitionSpec as P

F32 = jnp.float32
BF16 = jnp.bfloat16
SMALL = pltpu.CompilerParams(vmem_limit_bytes=8 * 1024 * 1024)
FREE = pl.CostEstimate(flops=0, bytes_accessed=0, transcendentals=0)
SKEW = 4
PAD = 16


def halves(value):
    high = value.astype(BF16)
    return high, (value - high.astype(F32)).astype(BF16)


def position(shape, dim, own, rim, reach, odd):
    at = lax.broadcasted_iota(jnp.int32, shape, dim)
    outside = 4 * own + 4 * rim
    step = jnp.where(at < own + rim, at - own, at - own - rim)
    above = own + step
    below = step - reach
    first = jnp.where(odd, below, above)
    second = jnp.where(odd, above, below)
    place = jnp.where(at < own + rim, first, second)
    place = jnp.where(step < reach, place, outside)
    return jnp.where(at < own, at, place)


def matrices(taps, parity, _, x_blur, x_back, y_blur, y_back, z_blur, z_back):
    views, _, count = taps.shape
    half = count // 2
    planes = x_blur.shape[0] // views
    wide = x_back.shape[0]
    width, slab = y_blur.shape[1], y_back.shape[1]
    depth = z_blur.shape[1] // 2
    odd_x, odd_y = parity[0] % 2 == 1, parity[1] % 2 == 1

    def pick(view, axis, offset):
        total = jnp.zeros(offset.shape, F32)
        for step in range(count):
            total = jnp.where(offset == step, taps[view, axis, step], total)
        return halves(total)

    def index(shape, dim):
        return lax.broadcasted_iota(jnp.int32, shape, dim)

    def tripled(high, low):
        return jnp.concatenate([high, high, low], axis=1)

    highs, lows = [], []
    for view in range(views):
        shape = (planes, wide)
        at = position(shape, 1, planes, PAD, half, odd_x)
        high, low = pick(view, 0, at - index(shape, 0) + half)
        x_blur[view * planes : (view + 1) * planes] = tripled(high, low)
        shape = (wide, planes)
        at = position(shape, 0, planes, PAD, half, odd_x)
        high, low = pick(view, 0, at - index(shape, 1) + half)
        highs.append(high)
        lows.append(low)
        shape = (width, slab)
        at = position(shape, 1, width, PAD, PAD, odd_y)
        y_blur[view] = tripled(*pick(view, 1, at - index(shape, 0) + half))
        shape = (slab, width)
        at = position(shape, 0, width, PAD, PAD, odd_y)
        y_back[view] = tripled(*pick(view, 1, at - index(shape, 1) + half))
        shape = (depth, depth)
        offset = index(shape, 0) - index(shape, 1) + half
        for ref, at in ((z_blur, offset), (z_back, 2 * half - offset)):
            high, low = pick(view, 2, at)
            ref[view, :depth] = jnp.concatenate([high, low], axis=1)
            ref[view, depth:] = jnp.concatenate([high, jnp.zeros_like(low)], axis=1)
    x_back[...] = jnp.concatenate(highs + highs + lows, axis=1)


def bands(kernels, parity, planes, width, depth, after):
    views = kernels.shape[0]
    wide, slab = planes + 2 * PAD, width + 2 * PAD
    shapes = [
        (views * planes, 3 * wide),
        (wide, 3 * views * planes),
        (views, width, 3 * slab),
        (views, slab, 3 * width),
        (views, 2 * depth, 2 * depth),
        (views, 2 * depth, 2 * depth),
    ]
    return pl.pallas_call(
        matrices,
        out_shape=[jax.ShapeDtypeStruct(s, BF16) for s in shapes],
        in_specs=[pl.BlockSpec(memory_space=pltpu.SMEM)] * 2 + [LATER],
        compiler_params=SMALL,
        name="matrices",
    )(kernels, parity, after)


def dot(left, right):
    return jnp.dot(left, right, preferred_element_type=F32)


def fused(
    own, xa, xb, yc, yd, views, light_kept, light_got, x_blur, x_back, y_blur, y_back, z_blur, z_back, _,
    s_own, s_xa, s_xb, s_yc, s_yd, ext, mid,
):
    count = views.shape[0]
    planes, width, depth = own.shape[1:]
    reach = xa.shape[1]
    wide, slab = planes + 2 * PAD, width + 2 * PAD
    pitch = slab + SKEW
    blocks = ((0, planes, own, s_own, 0), (planes, reach, xa, s_xa, planes), (planes + PAD, reach, xb, s_xb, planes + reach))

    def stacked(value):
        high, low = halves(value)
        return jnp.concatenate([high, low, high], axis=0)

    for start, size, ref, _, at in blocks:
        for i in range(size):
            base = (start + i) * pitch
            ext[base : base + width] = ref[0, i]
            ext[base + width : base + width + PAD] = yc[0, at + i]
            ext[base + width + PAD : base + slab] = yd[0, at + i]
    for plane in (planes + reach, planes + PAD + reach):
        ext[plane * pitch : plane * pitch + slab] = jnp.zeros((slab, depth), F32)

    rows = count * planes
    for y in range(0, slab, 2):
        pair = [stacked(ext[pl.ds(y + side, wide, stride=pitch), :]) for side in range(2)]
        out = dot(x_blur[...], jnp.concatenate(pair, axis=1))
        for side in range(2):
            mid[pl.ds(y + side, rows, stride=pitch), :] = out[:, side * depth : (side + 1) * depth]

    def through(value, matrix):
        high, low = halves(value)
        out = dot(jnp.concatenate([high, low], axis=1), matrix)
        return out[:, :depth] + out[:, depth:]

    def alone(view, matrix, values):
        outs = []
        for i in range(0, planes, 2):
            pair = jnp.concatenate([stacked(values[i]), stacked(values[i + 1])], axis=1)
            out = dot(matrix, pair)
            outs += [out[:, :depth], out[:, depth:]]
        return outs

    fields = []
    for view in range(count):
        bases = [(view * planes + i) * pitch for i in range(planes)]
        values = [mid[base : base + slab] for base in bases]
        fields.append(jnp.concatenate(alone(view, y_blur[view], values), axis=0))
    fields = [through(fields[view], z_blur[view]) for view in range(count)]
    ratios = []
    for view in range(count):
        light = (light_kept[view] + light_got[view])[None]
        field = fields[view].reshape(planes, width, depth)
        ratio = light * views[view, 0] / (light * field + 0.05)
        ratios.append(ratio.reshape(planes * width, depth))
    backs = [through(ratios[view], z_back[view]) for view in range(count)]
    for view in range(count):
        values = [backs[view][i * width : (i + 1) * width] for i in range(planes)]
        for i, out in enumerate(alone(view, y_back[view], values)):
            base = (view * planes + i) * pitch
            mid[base : base + slab] = out

    for y in range(0, slab, 2):
        pair = [stacked(mid[pl.ds(y + side, rows, stride=pitch), :]) for side in range(2)]
        out = dot(x_back[...], jnp.concatenate(pair, axis=1))
        for side in range(2):
            ext[pl.ds(y + side, wide, stride=pitch), :] = out[:, side * depth : (side + 1) * depth]

    for start, size, _, ref, at in blocks:
        for i in range(size):
            base = (start + i) * pitch
            ref[0, i] = ext[base : base + width]
            s_yc[0, at + i] = ext[base + width : base + width + PAD]
            s_yd[0, at + i] = ext[base + width + PAD : base + slab]


def brick(channel, estimate, xa, xb, yc, yd, views, lights, mats, after):
    count = views.shape[0]
    planes, width, depth = estimate.shape[1:]
    reach = xa.shape[1]
    total = planes + 2 * reach
    wide, slab = planes + 2 * PAD, width + 2 * PAD

    shapes = [(1, planes, width, depth)] + [(1, reach, width, depth)] * 2 + [(1, total, PAD, depth)] * 2
    return pl.pallas_call(
        fused,
        grid=(1,),
        out_shape=[jax.ShapeDtypeStruct(s, F32) for s in shapes],
        in_specs=[
            pl.BlockSpec((1, planes, width, depth), lambda i: (channel, 0, 0, 0)),
            whole(xa), whole(xb), whole(yc), whole(yd),
            pl.BlockSpec((count, 1, planes, width, depth), lambda i: (0, channel, 0, 0, 0)),
        ] + [whole(m) for m in (*lights, *mats)] + [LATER],
        out_specs=[pl.BlockSpec(s, lambda i: (0,) * 4) for s in shapes],
        scratch_shapes=[
            pltpu.VMEM((wide * (slab + SKEW), depth), F32),
            pltpu.VMEM((count * planes * (slab + SKEW), depth), F32),
        ],
        compiler_params=pltpu.CompilerParams(vmem_limit_bytes=24 * 1024 * 1024),
        name="brick%d" % channel,
    )(estimate, xa, xb, yc, yd, views, *lights, *mats, after)


def trade(value, axis, first):
    count = lax.axis_size(axis)
    pairs = []
    for low in range(0 if first else 1, count - 1, 2):
        pairs += [(low, low + 1), (low + 1, low)]
    return lax.ppermute(value, axis, pairs)


def whole(array):
    return pl.BlockSpec(array.shape, lambda i: (0,) * len(array.shape))


SCALARS = pl.BlockSpec(memory_space=pltpu.SMEM)
LATER = pl.BlockSpec(memory_space=pl.ANY)


def one_channel(array, channel):
    return pl.BlockSpec((1,) + array.shape[1:], lambda i: (channel, 0, 0, 0))


def call(body, name, ins, outs, deps=(), **more):
    count = len(ins)

    def kernel(*refs):
        body(*refs[:count], *refs[count + len(deps) :])

    out = pl.pallas_call(
        kernel,
        grid=(1,),
        out_shape=[jax.ShapeDtypeStruct(s, F32) for s in outs],
        in_specs=[spec for spec, _ in ins] + [LATER] * len(deps),
        out_specs=[pl.BlockSpec(s, lambda i, n=len(s): (0,) * n) for s in outs],
        compiler_params=SMALL,
        name=name,
        **more,
    )
    return out(*[array for _, array in ins], *deps)


def mask_profiles(cols, place, owners, profile, estimate, deps):
    _, _, count, _, depth = profile.shape
    width = estimate.shape[2]
    shape = (count, cols // 2, width, depth)

    def body(place, owners, profile, kept, sent):
        bit = place[1] % 2
        for view in range(count):
            valid = owners[view, place[0]] == place[1]
            for block in range(cols // 2):
                for ref, side in ((kept, bit), (sent, 1 - bit)):
                    start = pl.multiple_of((2 * block + side) * width, width)
                    value = profile[0, 0, view, pl.ds(start, width), :]
                    ref[view, block] = jnp.where(valid, value, 0.0)

    return call(
        body, "mask_profiles",
        [(SCALARS, place), (SCALARS, owners), (whole(profile), profile)], [shape] * 2, deps,
    )


def halve_profiles(step, place, kept, got, deps):
    count, blocks, width, depth = kept.shape
    shape = (count, blocks // 2, width, depth)

    def body(place, kept, got, out_kept, out_sent):
        bit = place[1] // step % 2
        for view in range(count):
            for block in range(blocks // 2):
                for ref, side in ((out_kept, bit), (out_sent, 1 - bit)):
                    at = 2 * block + side
                    ref[view, block] = kept[view, at] + got[view, at]

    return call(
        body, "halve_profiles%d" % step,
        [(SCALARS, place), (whole(kept), kept), (whole(got), got)], [shape] * 2, deps,
    )


def pack_planes(place, estimate, reach):
    channels, planes, width, depth = estimate.shape

    def body(place, own, *outs):
        odd = place[0] % 2
        for channel in range(channels):
            for out, side in zip(outs[2 * channel :], (1 - odd, odd)):
                out[0] = own[channel, pl.ds((planes - reach) * side, reach)]

    return call(
        body, "pack_planes", [(SCALARS, place), (whole(estimate), estimate)],
        [(1, reach, width, depth)] * (2 * channels),
    )


def row_starts(place, width):
    odd = place[1] % 2
    starts = ((width - PAD) * (1 - odd), (width - PAD) * odd)
    return tuple(pl.ds(pl.multiple_of(start, PAD), PAD) for start in starts)


def pack_rows(channel, place, estimate, xa, xb, deps):
    _, planes, width, depth = estimate.shape
    reach = xa.shape[1]

    def body(place, own, xa, xb, first, second):
        for out, rows in zip((first, second), row_starts(place, width)):
            out[0, :planes] = own[0, :, rows, :]
            out[0, planes : planes + reach] = xa[0, :, rows, :]
            out[0, planes + reach :] = xb[0, :, rows, :]

    return call(
        body, "pack_rows%d" % channel,
        [(SCALARS, place), (one_channel(estimate, channel), estimate), (whole(xa), xa), (whole(xb), xb)],
        [(1, planes + 2 * reach, PAD, depth)] * 2, deps,
    )


def add_rows(channel, place, s_xa, s_xb, rc, rd, deps):
    reach, width = s_xa.shape[1:3]
    base = rc.shape[1] - 2 * reach

    def body(place, s_xa, s_xb, rc, rd, first, second):
        first[...] = s_xa[...]
        second[...] = s_xb[...]
        for got, rows in zip((rc, rd), row_starts(place, width)):
            first[0, :, rows, :] += got[0, base : base + reach]
            second[0, :, rows, :] += got[0, base + reach :]

    return call(
        body, "add_rows%d" % channel,
        [(SCALARS, place)] + [(whole(a), a) for a in (s_xa, s_xb, rc, rd)], [s_xa.shape] * 2, deps,
    )


def finish(channel, views, place, estimate, s_own, rc, rd, qa, qb, done, deps):
    planes, width = s_own.shape[1:3]
    reach = qa.shape[1]

    def own_planes(array):
        return pl.BlockSpec((1, planes) + array.shape[2:], lambda i: (0,) * 4)

    def body(place, estimate, s_own, rc, rd, qa, qb, *rest):
        if channel == 1:
            qa, qb = qb, qa
        out = rest[-1]
        out[...] = s_own[...]
        for got, rows in zip((rc, rd), row_starts(place, width)):
            out[0, :, rows, :] += got[0]
        odd = place[0] % 2
        out[0, pl.ds((planes - reach) * (1 - odd), reach)] += qa[0]
        out[0, pl.ds((planes - reach) * odd, reach)] += qb[0]
        out[...] = estimate[...] * out[...] / views

    more = [] if done is None else [done]
    ends = [qb, qa] if channel == 1 else [qa, qb]
    ins = [place, estimate, s_own, rc, rd, *ends] + more + list(deps)
    return pl.pallas_call(
        body,
        grid=(1,),
        out_shape=jax.ShapeDtypeStruct(estimate.shape, F32),
        in_specs=[
            SCALARS, one_channel(estimate, channel), whole(s_own), own_planes(rc), own_planes(rd),
            whole(qa), whole(qb),
        ] + [LATER] * (len(more) + len(deps)),
        out_specs=one_channel(estimate, channel),
        input_output_aliases={7: 0} if more else {},
        compiler_params=SMALL,
        name="finish%d" % channel,
    )(*ins)


def flip(value, axis, step):
    return lax.ppermute(value, axis, [(i, i ^ step) for i in range(lax.axis_size(axis))])


def shards(views, estimate, profiles, kernels, owners):
    channels, planes, width, depth = estimate.shape
    reach = kernels.shape[2] // 2
    cols = lax.axis_size("by")
    place = jnp.stack([lax.axis_index("bx"), lax.axis_index("by")]).astype(jnp.int32)
    odd = place[0] % 2
    packed = []
    for c in range(channels):
        for side in (1 - odd, odd):
            packed.append(lax.dynamic_slice_in_dim(estimate[c : c + 1], (planes - reach) * side, reach, axis=1))
    halo = []
    for c in range(channels):
        xb = trade(packed[2 * c + 1], "bx", False)
        halo.append((trade(packed[2 * c], "bx", True), xb))
    kept, sent = mask_profiles(cols, place, owners, profiles, estimate, (packed[0],))
    step, mats = 1, None
    while True:
        got = flip(sent, "by", step)
        step *= 2
        if step == cols:
            break
        kept, sent = halve_profiles(step, place, kept, got, () if mats is None else (mats[0],))
        if mats is None:
            mats = bands(kernels, place, planes, width, depth, sent)
    if mats is None:
        mats = bands(kernels, place, planes, width, depth, sent)
    lights = (kept.reshape(-1, width, depth), got.reshape(-1, width, depth))
    rims = []
    for c in range(channels):
        xa, xb = halo[c]
        yc, yd = pack_rows(c, place, estimate, xa, xb, (sent if c == 0 else got,))
        yd = trade(yd, "by", False)
        rims.append((yc, trade(yc, "by", True), yd))
    ends, sums, done, prev = [], kernels, None, ()
    for c in range(channels):
        _, yc, yd = rims[c]
        s_own, s_xa, s_xb, s_yc, s_yd = brick(c, estimate, *halo[c], yc, yd, views, lights, mats, sums)
        rd = trade(s_yd, "by", False)
        rc = trade(s_yc, "by", True)
        first, second = add_rows(c, place, s_xa, s_xb, rc, rd, prev)
        sums = kernels
        qb = trade(second, "bx", False)
        qa = trade(first, "bx", True)
        prev = ()
        ends.append((s_own, rc, rd, qa, qb))
    done = None
    for c in range(channels):
        done = finish(c, views.shape[0], place, estimate, *ends[c], done, (sums,))
    return done


def solution(mesh):
    placed = (
        P(None, None, "bx", "by", None),
        P(None, "bx", "by", None),
        P("bx", "by", None, None, None),
        P(),
        P(),
    )
    return jax.shard_map(
        shards, mesh=mesh, in_specs=placed, out_specs=P(None, "bx", "by", None), check_vma=False
    )
```

```python
import functools

import jax
import jax.numpy as jnp
from jax import lax
from jax.experimental import pallas as pl
from jax.experimental.pallas import tpu as pltpu
from jax.sharding import PartitionSpec as P

F32 = jnp.float32
BF16 = jnp.bfloat16
SMALL = pltpu.CompilerParams(vmem_limit_bytes=8 * 1024 * 1024)
FREE = pl.CostEstimate(flops=0, bytes_accessed=0, transcendentals=0)
SKEW = 4
PAD = 16


def halves(value):
    high = value.astype(BF16)
    return high, (value - high.astype(F32)).astype(BF16)


def position(shape, dim, own, rim, reach, odd):
    at = lax.broadcasted_iota(jnp.int32, shape, dim)
    outside = 4 * own + 4 * rim
    step = jnp.where(at < own + rim, at - own, at - own - rim)
    above = own + step
    below = step - reach
    first = jnp.where(odd, below, above)
    second = jnp.where(odd, above, below)
    place = jnp.where(at < own + rim, first, second)
    place = jnp.where(step < reach, place, outside)
    return jnp.where(at < own, at, place)


def matrices(taps, parity, _, x_blur, x_back, y_blur, y_back, z_blur, z_back):
    views, _, count = taps.shape
    half = count // 2
    planes = x_blur.shape[0] // views
    wide = x_back.shape[0]
    width, slab = y_blur.shape[1], y_back.shape[1]
    depth = z_blur.shape[1] // 2
    odd_x, odd_y = parity[0] % 2 == 1, parity[1] % 2 == 1

    def pick(view, axis, offset):
        total = jnp.zeros(offset.shape, F32)
        for step in range(count):
            total = jnp.where(offset == step, taps[view, axis, step], total)
        return halves(total)

    def index(shape, dim):
        return lax.broadcasted_iota(jnp.int32, shape, dim)

    def tripled(high, low):
        return jnp.concatenate([high, high, low], axis=1)

    highs, lows = [], []
    for view in range(views):
        shape = (planes, wide)
        at = position(shape, 1, planes, PAD, half, odd_x)
        high, low = pick(view, 0, at - index(shape, 0) + half)
        x_blur[view * planes : (view + 1) * planes] = tripled(high, low)
        shape = (wide, planes)
        at = position(shape, 0, planes, PAD, half, odd_x)
        high, low = pick(view, 0, at - index(shape, 1) + half)
        highs.append(high)
        lows.append(low)
        shape = (width, slab)
        at = position(shape, 1, width, PAD, PAD, odd_y)
        y_blur[view] = tripled(*pick(view, 1, at - index(shape, 0) + half))
        shape = (slab, width)
        at = position(shape, 0, width, PAD, PAD, odd_y)
        y_back[view] = tripled(*pick(view, 1, at - index(shape, 1) + half))
        shape = (depth, depth)
        offset = index(shape, 0) - index(shape, 1) + half
        for ref, at in ((z_blur, offset), (z_back, 2 * half - offset)):
            high, low = pick(view, 2, at)
            ref[view, :depth] = jnp.concatenate([high, low], axis=1)
            ref[view, depth:] = jnp.concatenate([high, jnp.zeros_like(low)], axis=1)
    x_back[...] = jnp.concatenate(highs + highs + lows, axis=1)


def bands(kernels, parity, planes, width, depth, after):
    views = kernels.shape[0]
    wide, slab = planes + 2 * PAD, width + 2 * PAD
    shapes = [
        (views * planes, 3 * wide),
        (wide, 3 * views * planes),
        (views, width, 3 * slab),
        (views, slab, 3 * width),
        (views, 2 * depth, 2 * depth),
        (views, 2 * depth, 2 * depth),
    ]
    return pl.pallas_call(
        matrices,
        out_shape=[jax.ShapeDtypeStruct(s, BF16) for s in shapes],
        in_specs=[pl.BlockSpec(memory_space=pltpu.SMEM)] * 2 + [LATER],
        compiler_params=SMALL,
        name="matrices",
    )(kernels, parity, after)


def dot(left, right):
    return jnp.dot(left, right, preferred_element_type=F32)


def fused(
    own, xa, xb, yc, yd, views, light_kept, light_got, x_blur, x_back, y_blur, y_back, z_blur, z_back, _,
    s_own, s_xa, s_xb, s_yc, s_yd, ext, mid,
):
    count = views.shape[0]
    planes, width, depth = own.shape[1:]
    reach = xa.shape[1]
    wide, slab = planes + 2 * PAD, width + 2 * PAD
    pitch = slab + SKEW
    blocks = ((0, planes, own, s_own, 0), (planes, reach, xa, s_xa, planes), (planes + PAD, reach, xb, s_xb, planes + reach))

    def stacked(value):
        high, low = halves(value)
        return jnp.concatenate([high, low, high], axis=0)

    for start, size, ref, _, at in blocks:
        for i in range(size):
            base = (start + i) * pitch
            ext[base : base + width] = ref[0, i]
            ext[base + width : base + width + PAD] = yc[0, at + i]
            ext[base + width + PAD : base + slab] = yd[0, at + i]
    for plane in (planes + reach, planes + PAD + reach):
        ext[plane * pitch : plane * pitch + slab] = jnp.zeros((slab, depth), F32)

    rows = count * planes
    for y in range(0, slab, 2):
        pair = [stacked(ext[pl.ds(y + side, wide, stride=pitch), :]) for side in range(2)]
        out = dot(x_blur[...], jnp.concatenate(pair, axis=1))
        for side in range(2):
            mid[pl.ds(y + side, rows, stride=pitch), :] = out[:, side * depth : (side + 1) * depth]

    def through(value, matrix):
        high, low = halves(value)
        out = dot(jnp.concatenate([high, low], axis=1), matrix)
        return out[:, :depth] + out[:, depth:]

    def alone(view, matrix, values):
        outs = []
        for i in range(0, planes, 2):
            pair = jnp.concatenate([stacked(values[i]), stacked(values[i + 1])], axis=1)
            out = dot(matrix, pair)
            outs += [out[:, :depth], out[:, depth:]]
        return outs

    fields = []
    for view in range(count):
        bases = [(view * planes + i) * pitch for i in range(planes)]
        values = [mid[base : base + slab] for base in bases]
        fields.append(jnp.concatenate(alone(view, y_blur[view], values), axis=0))
    fields = [through(fields[view], z_blur[view]) for view in range(count)]
    ratios = []
    for view in range(count):
        light = (light_kept[view] + light_got[view])[None]
        field = fields[view].reshape(planes, width, depth)
        ratio = light * views[view, 0] / (light * field + 0.05)
        ratios.append(ratio.reshape(planes * width, depth))
    backs = [through(ratios[view], z_back[view]) for view in range(count)]
    for view in range(count):
        values = [backs[view][i * width : (i + 1) * width] for i in range(planes)]
        for i, out in enumerate(alone(view, y_back[view], values)):
            base = (view * planes + i) * pitch
            mid[base : base + slab] = out

    for y in range(0, slab, 2):
        pair = [stacked(mid[pl.ds(y + side, rows, stride=pitch), :]) for side in range(2)]
        out = dot(x_back[...], jnp.concatenate(pair, axis=1))
        for side in range(2):
            ext[pl.ds(y + side, wide, stride=pitch), :] = out[:, side * depth : (side + 1) * depth]

    for start, size, _, ref, at in blocks:
        for i in range(size):
            base = (start + i) * pitch
            ref[0, i] = ext[base : base + width]
            s_yc[0, at + i] = ext[base + width : base + width + PAD]
            s_yd[0, at + i] = ext[base + width + PAD : base + slab]


def brick(channel, estimate, xa, xb, yc, yd, views, lights, mats, after):
    count = views.shape[0]
    planes, width, depth = estimate.shape[1:]
    reach = xa.shape[1]
    total = planes + 2 * reach
    wide, slab = planes + 2 * PAD, width + 2 * PAD

    shapes = [(1, planes, width, depth)] + [(1, reach, width, depth)] * 2 + [(1, total, PAD, depth)] * 2
    return pl.pallas_call(
        fused,
        grid=(1,),
        out_shape=[jax.ShapeDtypeStruct(s, F32) for s in shapes],
        in_specs=[
            pl.BlockSpec((1, planes, width, depth), lambda i: (channel, 0, 0, 0)),
            whole(xa), whole(xb), whole(yc), whole(yd),
            pl.BlockSpec((count, 1, planes, width, depth), lambda i: (0, channel, 0, 0, 0)),
        ] + [whole(m) for m in (*lights, *mats)] + [LATER],
        out_specs=[pl.BlockSpec(s, lambda i: (0,) * 4) for s in shapes],
        scratch_shapes=[
            pltpu.VMEM((wide * (slab + SKEW), depth), F32),
            pltpu.VMEM((count * planes * (slab + SKEW), depth), F32),
        ],
        compiler_params=pltpu.CompilerParams(vmem_limit_bytes=24 * 1024 * 1024),
        name="brick%d" % channel,
    )(estimate, xa, xb, yc, yd, views, *lights, *mats, after)


def trade(value, axis, first):
    count = lax.axis_size(axis)
    pairs = []
    for low in range(0 if first else 1, count - 1, 2):
        pairs += [(low, low + 1), (low + 1, low)]
    return lax.ppermute(value, axis, pairs)


def whole(array):
    return pl.BlockSpec(array.shape, lambda i: (0,) * len(array.shape))


SCALARS = pl.BlockSpec(memory_space=pltpu.SMEM)
LATER = pl.BlockSpec(memory_space=pl.ANY)


def one_channel(array, channel):
    return pl.BlockSpec((1,) + array.shape[1:], lambda i: (channel, 0, 0, 0))


def call(body, name, ins, outs, deps=(), **more):
    count = len(ins)

    def kernel(*refs):
        body(*refs[:count], *refs[count + len(deps) :])

    out = pl.pallas_call(
        kernel,
        grid=(1,),
        out_shape=[jax.ShapeDtypeStruct(s, F32) for s in outs],
        in_specs=[spec for spec, _ in ins] + [LATER] * len(deps),
        out_specs=[pl.BlockSpec(s, lambda i, n=len(s): (0,) * n) for s in outs],
        compiler_params=SMALL,
        name=name,
        **more,
    )
    return out(*[array for _, array in ins], *deps)


def mask_profiles(cols, place, owners, profile, estimate, deps):
    _, _, count, _, depth = profile.shape
    width = estimate.shape[2]
    shape = (count, cols // 2, width, depth)

    def body(place, owners, profile, kept, sent):
        bit = place[1] % 2
        for view in range(count):
            valid = owners[view, place[0]] == place[1]
            for block in range(cols // 2):
                for ref, side in ((kept, bit), (sent, 1 - bit)):
                    start = pl.multiple_of((2 * block + side) * width, width)
                    value = profile[0, 0, view, pl.ds(start, width), :]
                    ref[view, block] = jnp.where(valid, value, 0.0)

    return call(
        body, "mask_profiles",
        [(SCALARS, place), (SCALARS, owners), (whole(profile), profile)], [shape] * 2, deps,
    )


def halve_profiles(step, place, kept, got, deps):
    count, blocks, width, depth = kept.shape
    shape = (count, blocks // 2, width, depth)

    def body(place, kept, got, out_kept, out_sent):
        bit = place[1] // step % 2
        for view in range(count):
            for block in range(blocks // 2):
                for ref, side in ((out_kept, bit), (out_sent, 1 - bit)):
                    at = 2 * block + side
                    ref[view, block] = kept[view, at] + got[view, at]

    return call(
        body, "halve_profiles%d" % step,
        [(SCALARS, place), (whole(kept), kept), (whole(got), got)], [shape] * 2, deps,
    )


def pack_planes(place, estimate, reach):
    channels, planes, width, depth = estimate.shape

    def body(place, own, *outs):
        odd = place[0] % 2
        for channel in range(channels):
            for out, side in zip(outs[2 * channel :], (1 - odd, odd)):
                out[0] = own[channel, pl.ds((planes - reach) * side, reach)]

    return call(
        body, "pack_planes", [(SCALARS, place), (whole(estimate), estimate)],
        [(1, reach, width, depth)] * (2 * channels),
    )


def row_starts(place, width):
    odd = place[1] % 2
    starts = ((width - PAD) * (1 - odd), (width - PAD) * odd)
    return tuple(pl.ds(pl.multiple_of(start, PAD), PAD) for start in starts)


def pack_rows(channel, place, estimate, xa, xb, deps):
    _, planes, width, depth = estimate.shape
    reach = xa.shape[1]

    def body(place, own, xa, xb, first, second):
        for out, rows in zip((first, second), row_starts(place, width)):
            out[0, :planes] = own[0, :, rows, :]
            out[0, planes : planes + reach] = xa[0, :, rows, :]
            out[0, planes + reach :] = xb[0, :, rows, :]

    return call(
        body, "pack_rows%d" % channel,
        [(SCALARS, place), (one_channel(estimate, channel), estimate), (whole(xa), xa), (whole(xb), xb)],
        [(1, planes + 2 * reach, PAD, depth)] * 2, deps,
    )


def add_rows(channel, place, s_xa, s_xb, rc, rd, deps):
    reach, width = s_xa.shape[1:3]
    base = rc.shape[1] - 2 * reach

    def body(place, s_xa, s_xb, rc, rd, first, second):
        first[...] = s_xa[...]
        second[...] = s_xb[...]
        for got, rows in zip((rc, rd), row_starts(place, width)):
            first[0, :, rows, :] += got[0, base : base + reach]
            second[0, :, rows, :] += got[0, base + reach :]

    return call(
        body, "add_rows%d" % channel,
        [(SCALARS, place)] + [(whole(a), a) for a in (s_xa, s_xb, rc, rd)], [s_xa.shape] * 2, deps,
    )


def finish(channel, views, place, estimate, s_own, rc, rd, qa, qb, done, deps):
    planes, width = s_own.shape[1:3]
    reach = qa.shape[1]

    def own_planes(array):
        return pl.BlockSpec((1, planes) + array.shape[2:], lambda i: (0,) * 4)

    def body(place, estimate, s_own, rc, rd, qa, qb, *rest):
        if channel == 1:
            qa, qb = qb, qa
        out = rest[-1]
        odd, cross = place[0] % 2, place[1] % 2 == 1
        gap = planes - reach
        for i in range(planes):
            total = s_own[0, i]
            low = jnp.where(cross, rc[0, i], rd[0, i])
            high = jnp.where(cross, rd[0, i], rc[0, i])
            total = total + jnp.concatenate([low, high], axis=0)
            for got, start in ((qa, gap * (1 - odd)), (qb, gap * odd)):
                at = i - start
                inside = jnp.logical_and(at >= 0, at < reach)
                value = got[0, jnp.clip(at, 0, reach - 1)]
                total = total + jnp.where(inside, value, 0.0)
            out[0, i] = estimate[0, i] * total / views

    more = [] if done is None else [done]
    ends = [qb, qa] if channel == 1 else [qa, qb]
    ins = [place, estimate, s_own, rc, rd, *ends] + more + list(deps)
    return pl.pallas_call(
        body,
        grid=(1,),
        out_shape=jax.ShapeDtypeStruct(estimate.shape, F32),
        in_specs=[
            SCALARS, one_channel(estimate, channel), whole(s_own), own_planes(rc), own_planes(rd),
            whole(qa), whole(qb),
        ] + [LATER] * (len(more) + len(deps)),
        out_specs=one_channel(estimate, channel),
        input_output_aliases={7: 0} if more else {},
        compiler_params=SMALL,
        name="finish%d" % channel,
    )(*ins)


def flip(value, axis, step):
    return lax.ppermute(value, axis, [(i, i ^ step) for i in range(lax.axis_size(axis))])


def shards(views, estimate, profiles, kernels, owners):
    channels, planes, width, depth = estimate.shape
    reach = kernels.shape[2] // 2
    cols = lax.axis_size("by")
    place = jnp.stack([lax.axis_index("bx"), lax.axis_index("by")]).astype(jnp.int32)
    odd = place[0] % 2
    packed = []
    for c in range(channels):
        for side in (1 - odd, odd):
            packed.append(lax.dynamic_slice_in_dim(estimate[c : c + 1], (planes - reach) * side, reach, axis=1))
    halo = []
    for c in range(channels):
        xb = trade(packed[2 * c + 1], "bx", False)
        halo.append((trade(packed[2 * c], "bx", True), xb))
    kept, sent = mask_profiles(cols, place, owners, profiles, estimate, (packed[0],))
    step, mats = 1, None
    while True:
        got = flip(sent, "by", step)
        step *= 2
        if step == cols:
            break
        kept, sent = halve_profiles(step, place, kept, got, () if mats is None else (mats[0],))
        if mats is None:
            mats = bands(kernels, place, planes, width, depth, sent)
    if mats is None:
        mats = bands(kernels, place, planes, width, depth, sent)
    lights = (kept.reshape(-1, width, depth), got.reshape(-1, width, depth))
    rims = []
    for c in range(channels):
        xa, xb = halo[c]
        yc, yd = pack_rows(c, place, estimate, xa, xb, (sent if c == 0 else got,))
        yd = trade(yd, "by", False)
        rims.append((yc, trade(yc, "by", True), yd))
    ends, sums, done, prev = [], kernels, None, ()
    for c in range(channels):
        _, yc, yd = rims[c]
        s_own, s_xa, s_xb, s_yc, s_yd = brick(c, estimate, *halo[c], yc, yd, views, lights, mats, sums)
        rd = trade(s_yd, "by", False)
        rc = trade(s_yc, "by", True)
        first, second = add_rows(c, place, s_xa, s_xb, rc, rd, prev)
        sums = kernels
        qb = trade(second, "bx", False)
        qa = trade(first, "bx", True)
        prev = ()
        ends.append((s_own, rc, rd, qa, qb))
    done = None
    for c in range(channels):
        done = finish(c, views.shape[0], place, estimate, *ends[c], done, (sums,))
    return done


def solution(mesh):
    placed = (
        P(None, None, "bx", "by", None),
        P(None, "bx", "by", None),
        P("bx", "by", None, None, None),
        P(),
        P(),
    )
    return jax.shard_map(
        shards, mesh=mesh, in_specs=placed, out_specs=P(None, "bx", "by", None), check_vma=False
    )
```

```python
import functools

import jax
import jax.numpy as jnp
from jax import lax
from jax.experimental import pallas as pl
from jax.experimental.pallas import tpu as pltpu
from jax.sharding import PartitionSpec as P

F32 = jnp.float32
BF16 = jnp.bfloat16
SMALL = pltpu.CompilerParams(vmem_limit_bytes=8 * 1024 * 1024)
FREE = pl.CostEstimate(flops=0, bytes_accessed=0, transcendentals=0)
SKEW = 4
PAD = 16


def halves(value):
    high = value.astype(BF16)
    return high, (value - high.astype(F32)).astype(BF16)


def position(shape, dim, own, rim, reach, odd):
    at = lax.broadcasted_iota(jnp.int32, shape, dim)
    outside = 4 * own + 4 * rim
    step = jnp.where(at < own + rim, at - own, at - own - rim)
    above = own + step
    below = step - reach
    first = jnp.where(odd, below, above)
    second = jnp.where(odd, above, below)
    place = jnp.where(at < own + rim, first, second)
    place = jnp.where(step < reach, place, outside)
    return jnp.where(at < own, at, place)


def matrices(taps, parity, _, x_blur, x_back, y_blur, y_back, z_blur, z_back):
    views, _, count = taps.shape
    half = count // 2
    planes = x_blur.shape[0] // views
    wide = x_back.shape[0]
    width, slab = y_blur.shape[1], y_back.shape[1]
    depth = z_blur.shape[1] // 2
    odd_x, odd_y = parity[0] % 2 == 1, parity[1] % 2 == 1

    def pick(view, axis, offset):
        total = jnp.zeros(offset.shape, F32)
        for step in range(count):
            total = jnp.where(offset == step, taps[view, axis, step], total)
        return halves(total)

    def index(shape, dim):
        return lax.broadcasted_iota(jnp.int32, shape, dim)

    def tripled(high, low):
        return jnp.concatenate([high, high, low], axis=1)

    highs, lows = [], []
    for view in range(views):
        shape = (planes, wide)
        at = position(shape, 1, planes, PAD, half, odd_x)
        high, low = pick(view, 0, at - index(shape, 0) + half)
        x_blur[view * planes : (view + 1) * planes] = tripled(high, low)
        shape = (wide, planes)
        at = position(shape, 0, planes, PAD, half, odd_x)
        high, low = pick(view, 0, at - index(shape, 1) + half)
        highs.append(high)
        lows.append(low)
        shape = (width, slab)
        at = position(shape, 1, width, PAD, PAD, odd_y)
        y_blur[view] = tripled(*pick(view, 1, at - index(shape, 0) + half))
        shape = (slab, width)
        at = position(shape, 0, width, PAD, PAD, odd_y)
        y_back[view] = tripled(*pick(view, 1, at - index(shape, 1) + half))
        shape = (depth, depth)
        offset = index(shape, 0) - index(shape, 1) + half
        for ref, at in ((z_blur, offset), (z_back, 2 * half - offset)):
            high, low = pick(view, 2, at)
            ref[view, :depth] = jnp.concatenate([high, low], axis=1)
            ref[view, depth:] = jnp.concatenate([high, jnp.zeros_like(low)], axis=1)
    x_back[...] = jnp.concatenate(highs + highs + lows, axis=1)


def bands(kernels, parity, planes, width, depth, after):
    views = kernels.shape[0]
    wide, slab = planes + 2 * PAD, width + 2 * PAD
    shapes = [
        (views * planes, 3 * wide),
        (wide, 3 * views * planes),
        (views, width, 3 * slab),
        (views, slab, 3 * width),
        (views, 2 * depth, 2 * depth),
        (views, 2 * depth, 2 * depth),
    ]
    return pl.pallas_call(
        matrices,
        out_shape=[jax.ShapeDtypeStruct(s, BF16) for s in shapes],
        in_specs=[pl.BlockSpec(memory_space=pltpu.SMEM)] * 2 + [LATER],
        compiler_params=SMALL,
        name="matrices",
    )(kernels, parity, after)


def dot(left, right):
    return jnp.dot(left, right, preferred_element_type=F32)


def fused(
    own, xa, xb, yc, yd, views, light_kept, light_got, x_blur, x_back, y_blur, y_back, z_blur, z_back, _,
    s_own, s_xa, s_xb, s_yc, s_yd, ext, mid,
):
    count = views.shape[0]
    planes, width, depth = own.shape[1:]
    reach = xa.shape[1]
    wide, slab = planes + 2 * PAD, width + 2 * PAD
    pitch = slab + SKEW
    blocks = ((0, planes, own, s_own, 0), (planes, reach, xa, s_xa, planes), (planes + PAD, reach, xb, s_xb, planes + reach))

    def stacked(value):
        high, low = halves(value)
        return jnp.concatenate([high, low, high], axis=0)

    for start, size, ref, _, at in blocks:
        for i in range(size):
            base = (start + i) * pitch
            ext[base : base + width] = ref[0, i]
            ext[base + width : base + width + PAD] = yc[0, at + i]
            ext[base + width + PAD : base + slab] = yd[0, at + i]
    for plane in (planes + reach, planes + PAD + reach):
        ext[plane * pitch : plane * pitch + slab] = jnp.zeros((slab, depth), F32)

    rows = count * planes
    for y in range(0, slab, 2):
        pair = [stacked(ext[pl.ds(y + side, wide, stride=pitch), :]) for side in range(2)]
        out = dot(x_blur[...], jnp.concatenate(pair, axis=1))
        for side in range(2):
            mid[pl.ds(y + side, rows, stride=pitch), :] = out[:, side * depth : (side + 1) * depth]

    def through(value, matrix):
        high, low = halves(value)
        out = dot(jnp.concatenate([high, low], axis=1), matrix)
        return out[:, :depth] + out[:, depth:]

    def alone(view, matrix, values):
        outs = []
        for i in range(0, planes, 2):
            pair = jnp.concatenate([stacked(values[i]), stacked(values[i + 1])], axis=1)
            out = dot(matrix, pair)
            outs += [out[:, :depth], out[:, depth:]]
        return outs

    fields = []
    for view in range(count):
        bases = [(view * planes + i) * pitch for i in range(planes)]
        values = [mid[base : base + slab] for base in bases]
        fields.append(jnp.concatenate(alone(view, y_blur[view], values), axis=0))
    fields = [through(fields[view], z_blur[view]) for view in range(count)]
    ratios = []
    for view in range(count):
        light = (light_kept[view] + light_got[view])[None]
        field = fields[view].reshape(planes, width, depth)
        ratio = light * views[view, 0] / (light * field + 0.05)
        ratios.append(ratio.reshape(planes * width, depth))
    backs = [through(ratios[view], z_back[view]) for view in range(count)]
    for view in range(count):
        values = [backs[view][i * width : (i + 1) * width] for i in range(planes)]
        for i, out in enumerate(alone(view, y_back[view], values)):
            base = (view * planes + i) * pitch
            mid[base : base + slab] = out

    for y in range(0, slab, 2):
        pair = [stacked(mid[pl.ds(y + side, rows, stride=pitch), :]) for side in range(2)]
        out = dot(x_back[...], jnp.concatenate(pair, axis=1))
        for side in range(2):
            ext[pl.ds(y + side, wide, stride=pitch), :] = out[:, side * depth : (side + 1) * depth]

    for start, size, _, ref, at in blocks:
        for i in range(size):
            base = (start + i) * pitch
            ref[0, i] = ext[base : base + width]
            s_yc[0, at + i] = ext[base + width : base + width + PAD]
            s_yd[0, at + i] = ext[base + width + PAD : base + slab]


def brick(channel, estimate, xa, xb, yc, yd, views, lights, mats, after):
    count = views.shape[0]
    planes, width, depth = estimate.shape[1:]
    reach = xa.shape[1]
    total = planes + 2 * reach
    wide, slab = planes + 2 * PAD, width + 2 * PAD

    shapes = [(1, planes, width, depth)] + [(1, reach, width, depth)] * 2 + [(1, total, PAD, depth)] * 2
    return pl.pallas_call(
        fused,
        grid=(1,),
        out_shape=[jax.ShapeDtypeStruct(s, F32) for s in shapes],
        in_specs=[
            pl.BlockSpec((1, planes, width, depth), lambda i: (channel, 0, 0, 0)),
            whole(xa), whole(xb), whole(yc), whole(yd),
            pl.BlockSpec((count, 1, planes, width, depth), lambda i: (0, channel, 0, 0, 0)),
        ] + [whole(m) for m in (*lights, *mats)] + [LATER],
        out_specs=[pl.BlockSpec(s, lambda i: (0,) * 4) for s in shapes],
        scratch_shapes=[
            pltpu.VMEM((wide * (slab + SKEW), depth), F32),
            pltpu.VMEM((count * planes * (slab + SKEW), depth), F32),
        ],
        compiler_params=pltpu.CompilerParams(vmem_limit_bytes=24 * 1024 * 1024),
        name="brick%d" % channel,
    )(estimate, xa, xb, yc, yd, views, *lights, *mats, after)


def trade(value, axis, first):
    count = lax.axis_size(axis)
    pairs = []
    for low in range(0 if first else 1, count - 1, 2):
        pairs += [(low, low + 1), (low + 1, low)]
    return lax.ppermute(value, axis, pairs)


def whole(array):
    return pl.BlockSpec(array.shape, lambda i: (0,) * len(array.shape))


SCALARS = pl.BlockSpec(memory_space=pltpu.SMEM)
LATER = pl.BlockSpec(memory_space=pl.ANY)


def one_channel(array, channel):
    return pl.BlockSpec((1,) + array.shape[1:], lambda i: (channel, 0, 0, 0))


def call(body, name, ins, outs, deps=(), **more):
    count = len(ins)

    def kernel(*refs):
        body(*refs[:count], *refs[count + len(deps) :])

    out = pl.pallas_call(
        kernel,
        grid=(1,),
        out_shape=[jax.ShapeDtypeStruct(s, F32) for s in outs],
        in_specs=[spec for spec, _ in ins] + [LATER] * len(deps),
        out_specs=[pl.BlockSpec(s, lambda i, n=len(s): (0,) * n) for s in outs],
        compiler_params=SMALL,
        name=name,
        **more,
    )
    return out(*[array for _, array in ins], *deps)


def mask_profiles(cols, place, owners, profile, estimate, deps):
    _, _, count, _, depth = profile.shape
    width = estimate.shape[2]
    shape = (count, cols // 2, width, depth)

    def body(place, owners, profile, kept, sent):
        bit = place[1] % 2
        for view in range(count):
            valid = owners[view, place[0]] == place[1]
            for block in range(cols // 2):
                for ref, side in ((kept, bit), (sent, 1 - bit)):
                    start = pl.multiple_of((2 * block + side) * width, width)
                    value = profile[0, 0, view, pl.ds(start, width), :]
                    ref[view, block] = jnp.where(valid, value, 0.0)

    return call(
        body, "mask_profiles",
        [(SCALARS, place), (SCALARS, owners), (whole(profile), profile)], [shape] * 2, deps,
    )


def halve_profiles(step, place, kept, got, deps):
    count, blocks, width, depth = kept.shape
    shape = (count, blocks // 2, width, depth)

    def body(place, kept, got, out_kept, out_sent):
        bit = place[1] // step % 2
        for view in range(count):
            for block in range(blocks // 2):
                for ref, side in ((out_kept, bit), (out_sent, 1 - bit)):
                    at = 2 * block + side
                    ref[view, block] = kept[view, at] + got[view, at]

    return call(
        body, "halve_profiles%d" % step,
        [(SCALARS, place), (whole(kept), kept), (whole(got), got)], [shape] * 2, deps,
    )


def pack_planes(place, estimate, reach):
    channels, planes, width, depth = estimate.shape

    def body(place, own, *outs):
        odd = place[0] % 2
        for channel in range(channels):
            for out, side in zip(outs[2 * channel :], (1 - odd, odd)):
                out[0] = own[channel, pl.ds((planes - reach) * side, reach)]

    return call(
        body, "pack_planes", [(SCALARS, place), (whole(estimate), estimate)],
        [(1, reach, width, depth)] * (2 * channels),
    )


def row_starts(place, width):
    odd = place[1] % 2
    starts = ((width - PAD) * (1 - odd), (width - PAD) * odd)
    return tuple(pl.ds(pl.multiple_of(start, PAD), PAD) for start in starts)


def pack_rows(channel, place, estimate, xa, xb, deps):
    _, planes, width, depth = estimate.shape
    reach = xa.shape[1]

    def body(place, own, xa, xb, first, second):
        for out, rows in zip((first, second), row_starts(place, width)):
            out[0, :planes] = own[0, :, rows, :]
            out[0, planes : planes + reach] = xa[0, :, rows, :]
            out[0, planes + reach :] = xb[0, :, rows, :]

    return call(
        body, "pack_rows%d" % channel,
        [(SCALARS, place), (one_channel(estimate, channel), estimate), (whole(xa), xa), (whole(xb), xb)],
        [(1, planes + 2 * reach, PAD, depth)] * 2, deps,
    )


def add_rows(channel, place, s_xa, s_xb, rc, rd, deps):
    reach, width = s_xa.shape[1:3]
    base = rc.shape[1] - 2 * reach

    def body(place, s_xa, s_xb, rc, rd, first, second):
        for got, rows in zip((rc, rd), row_starts(place, width)):
            first[0, :, rows, :] = s_xa[0, :, rows, :] + got[0, base : base + reach]
            second[0, :, rows, :] = s_xb[0, :, rows, :] + got[0, base + reach :]

    return call(
        body, "add_rows%d" % channel,
        [(SCALARS, place)] + [(whole(a), a) for a in (s_xa, s_xb, rc, rd)], [s_xa.shape] * 2, deps,
    )


def finish(channel, views, place, estimate, s_own, rc, rd, qa, qb, done, deps):
    planes, width = s_own.shape[1:3]
    reach = qa.shape[1]

    def own_planes(array):
        return pl.BlockSpec((1, planes) + array.shape[2:], lambda i: (0,) * 4)

    def body(place, estimate, s_own, rc, rd, qa, qb, *rest):
        if channel == 1:
            qa, qb = qb, qa
        out = rest[-1]
        odd, cross = place[0] % 2, place[1] % 2 == 1
        gap = planes - reach
        for i in range(planes):
            total = s_own[0, i]
            low = jnp.where(cross, rc[0, i], rd[0, i])
            high = jnp.where(cross, rd[0, i], rc[0, i])
            total = total + jnp.concatenate([low, high], axis=0)
            for got, start in ((qa, gap * (1 - odd)), (qb, gap * odd)):
                at = i - start
                inside = jnp.logical_and(at >= 0, at < reach)
                value = got[0, jnp.clip(at, 0, reach - 1)]
                total = total + jnp.where(inside, value, 0.0)
            out[0, i] = estimate[0, i] * total / views

    more = [] if done is None else [done]
    ends = [qb, qa] if channel == 1 else [qa, qb]
    ins = [place, estimate, s_own, rc, rd, *ends] + more + list(deps)
    return pl.pallas_call(
        body,
        grid=(1,),
        out_shape=jax.ShapeDtypeStruct(estimate.shape, F32),
        in_specs=[
            SCALARS, one_channel(estimate, channel), whole(s_own), own_planes(rc), own_planes(rd),
            whole(qa), whole(qb),
        ] + [LATER] * (len(more) + len(deps)),
        out_specs=one_channel(estimate, channel),
        input_output_aliases={7: 0} if more else {},
        compiler_params=SMALL,
        name="finish%d" % channel,
    )(*ins)


def flip(value, axis, step):
    return lax.ppermute(value, axis, [(i, i ^ step) for i in range(lax.axis_size(axis))])


def shards(views, estimate, profiles, kernels, owners):
    channels, planes, width, depth = estimate.shape
    reach = kernels.shape[2] // 2
    cols = lax.axis_size("by")
    place = jnp.stack([lax.axis_index("bx"), lax.axis_index("by")]).astype(jnp.int32)
    odd = place[0] % 2
    packed = []
    for c in range(channels):
        for side in (1 - odd, odd):
            packed.append(lax.dynamic_slice_in_dim(estimate[c : c + 1], (planes - reach) * side, reach, axis=1))
    halo = []
    for c in range(channels):
        xb = trade(packed[2 * c + 1], "bx", False)
        halo.append((trade(packed[2 * c], "bx", True), xb))
    kept, sent = mask_profiles(cols, place, owners, profiles, estimate, (packed[0],))
    step, mats = 1, None
    while True:
        got = flip(sent, "by", step)
        step *= 2
        if step == cols:
            break
        kept, sent = halve_profiles(step, place, kept, got, () if mats is None else (mats[0],))
        if mats is None:
            mats = bands(kernels, place, planes, width, depth, sent)
    if mats is None:
        mats = bands(kernels, place, planes, width, depth, sent)
    lights = (kept.reshape(-1, width, depth), got.reshape(-1, width, depth))
    rims = []
    for c in range(channels):
        xa, xb = halo[c]
        yc, yd = pack_rows(c, place, estimate, xa, xb, (sent if c == 0 else got,))
        yd = trade(yd, "by", False)
        rims.append((yc, trade(yc, "by", True), yd))
    ends, sums, done, prev = [], kernels, None, ()
    for c in range(channels):
        _, yc, yd = rims[c]
        s_own, s_xa, s_xb, s_yc, s_yd = brick(c, estimate, *halo[c], yc, yd, views, lights, mats, sums)
        rd = trade(s_yd, "by", False)
        rc = trade(s_yc, "by", True)
        first, second = add_rows(c, place, s_xa, s_xb, rc, rd, prev)
        sums = kernels
        qb = trade(second, "bx", False)
        qa = trade(first, "bx", True)
        prev = ()
        ends.append((s_own, rc, rd, qa, qb))
    done = None
    for c in range(channels):
        done = finish(c, views.shape[0], place, estimate, *ends[c], done, (sums,))
    return done


def solution(mesh):
    placed = (
        P(None, None, "bx", "by", None),
        P(None, "bx", "by", None),
        P("bx", "by", None, None, None),
        P(),
        P(),
    )
    return jax.shard_map(
        shards, mesh=mesh, in_specs=placed, out_specs=P(None, "bx", "by", None), check_vma=False
    )
```
